32 devices in a mesh: groups: 2 (over y), adapter: 16 (over z, x, core).
Axes of the slice: x: 2, y: 2, z: 4, core: 2. Of those that a mesh axis runs over, the one named last changes fastest.
Arguments:
- hidden: bfloat16 [4096, 8192], P(('groups', 'adapter')), parts along dimension 0, may hold values from -6 to 6
- queries: bfloat16 [4096, 4096], P(('groups', 'adapter')), parts along dimension 0, may hold values from -6 to 6
- base_key_value: bfloat16 [4096, 1024], P(('groups', 'adapter')), parts along dimension 0, may hold values from -6 to 6
- key_value_cache: bfloat16 [4096, 16, 1024], P(('groups', 'adapter')), parts along dimension 0, may hold values from -6 to 6
- lengths: int32 [4096], P(('groups', 'adapter')), parts along dimension 0, may hold values from 2 to 16, as said below
- request_adapter_index: int32 [4096, 1], P(('groups', 'adapter')), parts along dimension 0, may hold values from 0 to 15; in each aligned block of 128 rows (0 to 127, 128 to 255, ...) at most 16 rows name the same one
- adapter_position_map: int32 [32], P('groups'), parts along dimension 0, may hold values from 0 to 15, each once
- adapter_down_weight: bfloat16 [32, 64, 8192], P(('groups', 'adapter')), parts along dimension 0, may hold values from -0.0625 to 0.0625
- adapter_up_weight: bfloat16 [32, 64, 1024], P(('groups', 'adapter')), parts along dimension 0, may hold values from -0.75 to 0.75
Outputs:
- attention: bfloat16 [4096, 4096], P(('groups', 'adapter')), parts along dimension 0
- written_key_value: bfloat16 [4096, 1024], P(('groups', 'adapter')), parts along dimension 0
The draws below stay inside these ranges and needn't reach their ends.
There are 2 independent parts, one for each index of `groups`. The reference program is written for one: setup_inputs(seed, part) draws one part's arguments, and reference() takes and returns one part's arrays. A program takes and returns all parts, laid end to end along the dimension named above; each array names one. Nothing has to cross between parts.
Inputs may be any that keep to these rules, and one draw needn't show every extreme that they name: `lengths`: some request has all 16 positions in use. `request_adapter_index`: the 128 requests of one device name one adapter at most 16 times; in some device one adapter is named exactly 16 times. `adapter_position_map`: A permutation of the adapters.
All inputs are finite; a program needn't handle non-finite values.
Results may differ from the reference program's by a relative error of at most 0.0073.
Values may be sent and summed in bfloat16 or wider, within the bound.
No kernel may reach another device: no remote copies, remote signals or barrier semaphores. Data moves between devices by JAX's collectives and lax.ppermute only.
A program may use at most 64 MiB of HBM per device.

```python
import math
import jax
import jax.numpy as jnp
import numpy as np
from jax import lax

MODEL_WIDTH = 8192
QUERY_HEADS = 32
KEY_VALUE_HEADS = 4
HEAD_SIZE = 128
ADAPTER_RANK = 64
CONTEXT_LENGTH = 16
DEVICE_REQUESTS = 128
REQUEST_TOTAL = 2048
ADAPTER_TOTAL = 16
MOST = 16
QW = 4096
KEY_VALUE_WIDTH = 1024
N_ADAPTER = 16


def draw_queries(key, part):
    key = jax.random.fold_in(key, 3)
    return jnp.clip(jax.random.normal(key, (REQUEST_TOTAL, QUERY_HEADS * HEAD_SIZE), jnp.float32), -6.0, 6.0).astype(jnp.bfloat16)


def draw_key_value_cache(key, part):
    key = jax.random.fold_in(key, 5)
    key_value_split = KEY_VALUE_HEADS * HEAD_SIZE
    return jnp.clip(jax.random.normal(key, (REQUEST_TOTAL, CONTEXT_LENGTH, 2 * key_value_split), jnp.float32), -6.0, 6.0).astype(jnp.bfloat16)


def draw_lengths(key, part):
    key = jax.random.fold_in(key, 7)
    value_key, spot_key = jax.random.split(key)
    drawn = jax.random.randint(value_key, (REQUEST_TOTAL,), 2, CONTEXT_LENGTH + 1)
    spot = jax.random.randint(spot_key, (), 0, REQUEST_TOTAL)
    return drawn.at[spot].set(CONTEXT_LENGTH).astype(jnp.int32)


def levels(own_key, dims, cuts, least, top_value):
    level, own = 1.0, jax.random.fold_in(own_key, 6)
    for dim, parts in cuts:
        draws = jnp.exp(jax.random.uniform(jax.random.fold_in(own, dim), (parts,), jnp.float32, least / len(cuts), top_value / len(cuts)))
        level = level * jnp.repeat(draws, dims[dim] // parts).reshape([-1 if axis == dim else 1 for axis in range(len(dims))])
    return level


def shared_out(own_key, own, number, rows, count, top, bound, skew):
    order = jax.random.permutation(own_key, count)
    packed, ordinary = shares(count, rows * top, bound, skew, True), shares(count, rows * top, bound, skew, False)
    places = jnp.arange(count)

    def named(sizes, rotation):
        used = int((sizes > 0).sum())
        fixed = max(1, used // 4)
        passed = fixed + (places - fixed + rotation * (used - fixed)) % max(1, count - fixed)
        return jnp.zeros((count,), jnp.int32).at[order[jnp.where(places < fixed, places, passed)]].set(jnp.asarray(sizes, jnp.int32))

    sizes = jnp.where(number % 4 == 0, named(packed, number // 4), named(ordinary, number - number // 4 - 1))
    mixed = jax.random.permutation(jax.random.fold_in(own, 3), count)
    donor, receiver = mixed[0:count // 2 * 2:2], mixed[1:count // 2 * 2:2]
    margin = jnp.minimum(sizes[donor] - 1, bound - sizes[receiver]) // 2
    margin = jnp.where((donor == order[0]) | (receiver == order[0]) | (sizes[receiver] == 0), 0, jnp.maximum(margin, 0))
    passed = jax.random.randint(jax.random.fold_in(own, 4), (count // 2,), 0, 1 << 20) % (margin + 1)
    sizes = sizes.at[donor].add(-passed).at[receiver].add(passed)
    items = jnp.searchsorted(jnp.cumsum(sizes), jnp.arange(rows * top), side="right").astype(jnp.int32)
    grid = items.reshape(top, rows).T
    grid = grid[jax.random.permutation(jax.random.fold_in(own, 1), rows)]
    rotation = jax.random.randint(jax.random.fold_in(own, 2), (rows, 1), 0, top)
    return jnp.take_along_axis(grid, (jnp.arange(top)[None, :] + rotation) % top, axis=1)


def shares(count, total, bound, lean, full):
    weights = [(1 << 20) // math.isqrt(rank ** lean) + 1 for rank in range(1, count + 1)]
    largest = bound if full else min(bound, max(-(-total // count), total * weights[0] // sum(weights)))
    least = 1 if total - largest >= count - 1 else 0
    holding, surplus = [largest] + [least] * (count - 1), total - largest - least * (count - 1)
    while surplus > 0:
        candidates = [i for i in range(1, count) if holding[i] < largest] or [i for i in range(1, count) if holding[i] < bound]
        mass, remaining = sum([weights[i] for i in candidates]), surplus
        for i in candidates:
            more = min(bound - holding[i], max(1, remaining * weights[i] // mass), surplus)
            holding[i] = holding[i] + more
            surplus = surplus - more
    return np.array(holding)


def noise(stream_key, extent, spread, most, pieces=(), kind=jnp.bfloat16):
    gain = levels(stream_key, extent, pieces, -0.22, 0.18) if pieces else 1.0
    values = jax.random.normal(stream_key, extent, jnp.float32) * spread * gain
    return jnp.minimum(jnp.maximum(values, -most), most).astype(kind)


def setup_inputs(seed: int = 0, part: int = 0) -> dict:
    key_of = jax.random.split(jax.random.key(seed), 10)
    own_keys = jax.random.split(jax.random.fold_in(key_of[9], part), 10)
    hidden = noise(own_keys[0], (REQUEST_TOTAL, MODEL_WIDTH), 1.0, 6.0, ((0, 16),))
    queries = draw_queries(jax.random.fold_in(jax.random.fold_in(key_of[9], part), 71), part)
    base_key_value = noise(own_keys[2], (REQUEST_TOTAL, KEY_VALUE_WIDTH), 1.0, 6.0, ((0, 16),))
    key_value_cache = draw_key_value_cache(jax.random.fold_in(jax.random.fold_in(key_of[9], part), 71), part)
    lengths = draw_lengths(jax.random.fold_in(jax.random.fold_in(key_of[9], part), 71), part)
    request_adapter_index_keys = jax.random.split(jax.random.fold_in(own_keys[5], 1), REQUEST_TOTAL // DEVICE_REQUESTS)
    request_adapter_index_turns = jax.random.permutation(jax.random.fold_in(own_keys[5], 3), REQUEST_TOTAL // DEVICE_REQUESTS)
    request_adapter_index = jax.vmap(lambda own, number: shared_out(jax.random.fold_in(own_keys[5], 2), own, number, DEVICE_REQUESTS, ADAPTER_TOTAL, 1, MOST, 2))(request_adapter_index_keys, request_adapter_index_turns).reshape((REQUEST_TOTAL, 1))
    adapter_position_map = jax.random.permutation(own_keys[6], ADAPTER_TOTAL).astype(jnp.int32)
    adapter_down_weight = noise(own_keys[7], (ADAPTER_TOTAL, ADAPTER_RANK, MODEL_WIDTH), MODEL_WIDTH ** -0.5, 0.0625, ((0, 16),))
    adapter_up_weight = noise(own_keys[8], (ADAPTER_TOTAL, ADAPTER_RANK, KEY_VALUE_WIDTH), ADAPTER_RANK ** -0.5, 0.75, ((0, 16),))
    return dict(hidden=hidden, queries=queries, base_key_value=base_key_value, key_value_cache=key_value_cache, lengths=lengths, request_adapter_index=request_adapter_index, adapter_position_map=adapter_position_map, adapter_down_weight=adapter_down_weight, adapter_up_weight=adapter_up_weight)


adapter_scale = 2.0
score_floor = -1e30


def adapter_weight_block(hidden_state_rows, slot_index_list, adapter_down_weight, adapter_up_weight):
    down_weight_rows = adapter_down_weight[slot_index_list].astype(jnp.float32)
    up_weight_rows = adapter_up_weight[slot_index_list].astype(jnp.float32)
    reduced_output = jnp.einsum('rd,rkd->rk', hidden_state_rows.astype(jnp.float32), down_weight_rows).astype(jnp.bfloat16)
    expanded_output = jnp.einsum('rk,rkc->rc', reduced_output.astype(jnp.float32), up_weight_rows)
    return (adapter_scale * expanded_output).astype(jnp.bfloat16)


def attend_block(query_vectors, cached_row_block, newest_rows, length_rows):
    row_total_count = query_vectors.shape[0]
    query_group_size = QUERY_HEADS // KEY_VALUE_HEADS
    key_value_split = KEY_VALUE_HEADS * HEAD_SIZE
    query_head_rows = query_vectors.astype(jnp.float32).reshape(row_total_count, KEY_VALUE_HEADS, query_group_size, HEAD_SIZE)
    cached_key_block = cached_row_block[:, :, :key_value_split].astype(jnp.float32).reshape(row_total_count, CONTEXT_LENGTH, KEY_VALUE_HEADS, HEAD_SIZE)
    cached_value_block = cached_row_block[:, :, key_value_split:].astype(jnp.float32).reshape(row_total_count, CONTEXT_LENGTH, KEY_VALUE_HEADS, HEAD_SIZE)
    newest_key = newest_rows[:, :key_value_split].astype(jnp.float32).reshape(row_total_count, KEY_VALUE_HEADS, HEAD_SIZE)
    newest_value = newest_rows[:, key_value_split:].astype(jnp.float32).reshape(row_total_count, KEY_VALUE_HEADS, HEAD_SIZE)
    score_scale = HEAD_SIZE ** -0.5
    cached = jnp.einsum('rhgd,rphd->rhgp', query_head_rows, cached_key_block) * score_scale
    in_range = jnp.arange(CONTEXT_LENGTH, dtype=jnp.int32)[None, :] < length_rows[:, None]
    cached = jnp.where(in_range[:, None, None, :], cached, score_floor)
    self_score = jnp.einsum('rhgd,rhd->rhg', query_head_rows, newest_key) * score_scale
    peak_score = jnp.maximum(jnp.max(cached, axis=-1), self_score)
    cached_exp = jnp.exp(cached - peak_score[..., None])
    self_exp = jnp.exp(self_score - peak_score)
    denominator = jnp.sum(cached_exp, axis=-1) + self_exp
    cached_weight = lax.optimization_barrier((cached_exp / denominator[..., None]).astype(jnp.bfloat16))
    self_weight = lax.optimization_barrier((self_exp / denominator).astype(jnp.bfloat16))
    mixed = jnp.einsum('rhgp,rphd->rhgd', cached_weight.astype(jnp.float32), cached_value_block)
    mixed = mixed + self_weight.astype(jnp.float32)[..., None] * newest_value[:, :, None, :]
    return mixed.reshape(row_total_count, QUERY_HEADS * HEAD_SIZE).astype(jnp.bfloat16)


def reference(hidden, queries, base_key_value, key_value_cache, lengths, request_adapter_index, adapter_position_map, adapter_down_weight, adapter_up_weight):
    slot_index_list = adapter_position_map[request_adapter_index[:, 0]].astype(jnp.int32)

    def single_block(block_pair):
        hidden_state_rows, slot_row_block = block_pair
        return adapter_weight_block(hidden_state_rows, slot_row_block, adapter_down_weight, adapter_up_weight)

    adapter_correction = lax.map(single_block, (hidden.reshape(N_ADAPTER, DEVICE_REQUESTS, MODEL_WIDTH), slot_index_list.reshape(N_ADAPTER, DEVICE_REQUESTS)))
    adapter_correction = adapter_correction.reshape(REQUEST_TOTAL, KEY_VALUE_WIDTH)
    written_key_value = (base_key_value.astype(jnp.float32) + adapter_correction.astype(jnp.float32)).astype(jnp.bfloat16)

    def attend_one(block_pack):
        query_vectors, cached_row_block, newest_rows, length_rows = block_pack
        return attend_block(query_vectors, cached_row_block, newest_rows, length_rows)

    attention = lax.map(attend_one, (queries.reshape(N_ADAPTER, DEVICE_REQUESTS, QW), key_value_cache.reshape(N_ADAPTER, DEVICE_REQUESTS, CONTEXT_LENGTH, KEY_VALUE_WIDTH), written_key_value.reshape(N_ADAPTER, DEVICE_REQUESTS, KEY_VALUE_WIDTH), lengths.reshape(N_ADAPTER, DEVICE_REQUESTS)))
    return attention.reshape(REQUEST_TOTAL, QW), written_key_value
```

```python
import functools

import jax
import jax.numpy as jnp
from jax import lax
from jax.experimental import pallas as pl
from jax.experimental.pallas import tpu as pltpu
from jax.sharding import PartitionSpec as P

QUERY_HEADS = 32
KEY_VALUE_HEADS = 4
HEAD_SIZE = 128
GROUP = QUERY_HEADS // KEY_VALUE_HEADS
SPLIT = KEY_VALUE_HEADS * HEAD_SIZE
PLANE = 4
COLS = 1024

adapter_scale = 2.0
score_floor = -1e30
score_scale = HEAD_SIZE ** (-0.5)

NT = (((1,), (1,)), ((), ()))


def slot_lookup(request_adapter, adapter_position_map):
    adapter_index = jnp.arange(adapter_position_map.shape[0], dtype=jnp.int32)
    matches = request_adapter[:, None] == adapter_index[None, :]
    return jnp.sum(jnp.where(matches, adapter_position_map[None, :], 0), axis=1)


def rank_in_slot(slot):
    order = jnp.arange(slot.shape[0], dtype=jnp.int32)
    same = slot[:, None] == slot[None, :]
    before = order[None, :] < order[:, None]
    return jnp.sum((same & before).astype(jnp.int32), axis=1)


def params(*semantics):
    return pltpu.CompilerParams(
        dimension_semantics=semantics, vmem_limit_bytes=40 * 1024 * 1024
    )


def cached_kernel(length_ref, q_ref, cache_ref, mixed_ref, log_ref):
    rows, context = cache_ref.shape[0], cache_ref.shape[1]
    keys = rows * context
    owner_q = lax.rem(lax.broadcasted_iota(jnp.int32, (GROUP * rows, keys), 0), rows)
    column = lax.broadcasted_iota(jnp.int32, (GROUP * rows, keys), 1)
    owner_k, position = column // context, lax.rem(column, context)
    lengths = jnp.concatenate([length_ref[...]] * GROUP, axis=0)
    included = (owner_q == owner_k) & (position < lengths)
    lane = lax.broadcasted_iota(jnp.int32, (rows, HEAD_SIZE), 1)
    logs = jnp.zeros((rows, HEAD_SIZE), jnp.float32)
    for head in range(KEY_VALUE_HEADS):
        first = head * GROUP
        q = jnp.concatenate(
            [
                q_ref[:, (first + g) * HEAD_SIZE : (first + g + 1) * HEAD_SIZE]
                for g in range(GROUP)
            ],
            axis=0,
        )
        k = cache_ref[:, :, head * HEAD_SIZE : (head + 1) * HEAD_SIZE].reshape(keys, HEAD_SIZE)
        v = cache_ref[
            :, :, SPLIT + head * HEAD_SIZE : SPLIT + (head + 1) * HEAD_SIZE
        ].reshape(keys, HEAD_SIZE)
        score = lax.dot_general(q, k, NT, preferred_element_type=jnp.float32) * score_scale
        score = jnp.where(included, score, score_floor)
        peak = jnp.max(score, axis=1, keepdims=True)
        weight = jnp.exp(score - peak)
        total = jnp.sum(weight, axis=1, keepdims=True)
        mixed = jnp.dot(weight.astype(jnp.bfloat16), v, preferred_element_type=jnp.float32)
        mixed = mixed / total
        log = peak + jnp.log(total)
        for g in range(GROUP):
            part = slice(g * rows, (g + 1) * rows)
            mixed_ref[:, (first + g) * HEAD_SIZE : (first + g + 1) * HEAD_SIZE] = mixed[part]
            logs = jnp.where(lane == first + g, log[part], logs)
    log_ref[...] = logs


def cached_attention(queries, cache, lengths):
    rows, context, width = cache.shape
    step = 16
    return pl.pallas_call(
        cached_kernel,
        grid=(rows // step,),
        in_specs=[
            pl.BlockSpec((step, 1), lambda i: (i, 0)),
            pl.BlockSpec((step, queries.shape[1]), lambda i: (i, 0)),
            pl.BlockSpec((step, context, width), lambda i: (i, 0, 0)),
        ],
        out_specs=[
            pl.BlockSpec((step, queries.shape[1]), lambda i: (i, 0)),
            pl.BlockSpec((step, HEAD_SIZE), lambda i: (i, 0)),
        ],
        out_shape=[
            jax.ShapeDtypeStruct(queries.shape, jnp.float32),
            jax.ShapeDtypeStruct((rows, HEAD_SIZE), jnp.float32),
        ],
        compiler_params=params("arbitrary"),
        cost_estimate=pl.CostEstimate(
            flops=2_000_000_000, bytes_accessed=30_000_000, transcendentals=1_000_000
        ),
        name="cached",
    )(lengths.reshape(rows, 1), queries, cache)


def finish_kernel(count, target_ref, base_ref, q_ref, mixed_ref, log_ref, *refs):
    pieces, (attention_ref, written_ref, place_ref) = refs[:count], refs[count:]
    head = pl.program_id(0)
    rows = base_ref.shape[0]

    @pl.when(head == 0)
    def _():
        spots = lax.broadcasted_iota(jnp.int32, place_ref.shape, 1)
        place_ref[...] = (spots == target_ref[...]).astype(jnp.float32).astype(jnp.bfloat16)

    def written(offset):
        columns = pl.ds(pl.multiple_of(offset, HEAD_SIZE), HEAD_SIZE)
        stack = jnp.concatenate([piece[:, columns] for piece in pieces], axis=0)
        delta = jnp.dot(place_ref[...], stack, preferred_element_type=jnp.float32)
        value = (base_ref[:, columns].astype(jnp.float32) + delta).astype(jnp.bfloat16)
        written_ref[:, columns] = value
        return value.astype(jnp.float32)

    new_key = written(head * HEAD_SIZE)
    new_value = written(SPLIT + head * HEAD_SIZE)
    lane = lax.broadcasted_iota(jnp.int32, (rows, HEAD_SIZE), 1)
    logs = log_ref[...]
    for g in range(GROUP):
        part = slice(g * HEAD_SIZE, (g + 1) * HEAD_SIZE)
        query = q_ref[:, part].astype(jnp.float32)
        score = jnp.sum(query * new_key, axis=1, keepdims=True) * score_scale
        log = jnp.sum(jnp.where(lane == head * GROUP + g, logs, 0.0), axis=1, keepdims=True)
        share = 1.0 / (1.0 + jnp.exp(score - log))
        out = new_value + share * (mixed_ref[:, part] - new_value)
        attention_ref[:, part] = out.astype(jnp.bfloat16)


def finish(target, base, queries, mixed, logs, pieces):
    rows = base.shape[0]
    wide = GROUP * HEAD_SIZE
    whole = lambda a: pl.BlockSpec(a.shape, lambda h: (0, 0))
    total = sum(piece.shape[0] for piece in pieces)
    target = target.reshape(rows, 1)
    return pl.pallas_call(
        functools.partial(finish_kernel, len(pieces)),
        grid=(KEY_VALUE_HEADS,),
        in_specs=[
            whole(target),
            whole(base),
            pl.BlockSpec((rows, wide), lambda h: (0, h)),
            pl.BlockSpec((rows, wide), lambda h: (0, h)),
            whole(logs),
        ]
        + [whole(piece) for piece in pieces],
        out_specs=[pl.BlockSpec((rows, wide), lambda h: (0, h)), whole(base)],
        out_shape=[
            jax.ShapeDtypeStruct(queries.shape, jnp.bfloat16),
            jax.ShapeDtypeStruct(base.shape, jnp.bfloat16),
        ],
        scratch_shapes=[pltpu.VMEM((rows, total), jnp.bfloat16)],
        compiler_params=params("arbitrary"),
        name="finish",
    )(target, base, queries, mixed, logs, *pieces)


def pack_kernel(capacity, target_ref, hidden_ref, *outs):
    rows = hidden_ref.shape[0]
    spots = 4 * PLANE * capacity
    spot = lax.broadcasted_iota(jnp.int32, (spots, rows), 0)
    place = (spot == target_ref[...]).astype(jnp.float32).astype(jnp.bfloat16)
    packed = jnp.dot(place, hidden_ref[...], preferred_element_type=jnp.float32)
    packed = packed.astype(jnp.bfloat16)
    start = 0
    for out in outs:
        out[...] = packed[start : start + out.shape[0]]
        start += out.shape[0]


def pack(target, hidden, capacity):
    rows, width = hidden.shape
    heights = [capacity] * PLANE + [3 * capacity] * PLANE
    return pl.pallas_call(
        functools.partial(pack_kernel, capacity),
        grid=(width // COLS,),
        in_specs=[
            pl.BlockSpec((1, rows), lambda c: (0, 0)),
            pl.BlockSpec((rows, COLS), lambda c: (0, c)),
        ],
        out_specs=[pl.BlockSpec((h, COLS), lambda c: (0, c)) for h in heights],
        out_shape=[jax.ShapeDtypeStruct((h, width), jnp.bfloat16) for h in heights],
        compiler_params=params("arbitrary"),
        name="pack",
    )(target.reshape(1, rows), hidden)


def expand(total, up):
    shrunk = total.astype(jnp.bfloat16)
    wide = jnp.dot(shrunk, up, preferred_element_type=jnp.float32)
    return (adapter_scale * wide).astype(jnp.bfloat16)


def early_kernel(capacity, inner_ref, *refs):
    first, rest = refs[:PLANE], refs[PLANE : 2 * PLANE]
    down_refs, up_refs = refs[2 * PLANE : 2 * PLANE + 3], refs[2 * PLANE + 3 : 2 * PLANE + 6]
    outs, totals = refs[2 * PLANE + 6 : 3 * PLANE + 6], refs[3 * PLANE + 6 :]
    step, steps = pl.program_id(0), pl.num_programs(0)
    inner = inner_ref[0] == 1

    def weights(three):
        own, outward, middle = three
        return outward[...], own[...], jnp.where(inner, middle[...], outward[...])

    stacks = [jnp.concatenate([r[...] for r in first], axis=0)]
    for slot in range(2):
        part = slice(slot * capacity, (slot + 1) * capacity)
        stacks.append(jnp.concatenate([r[part] for r in rest], axis=0))
    for total, stack, down in zip(totals, stacks, weights(down_refs)):
        product = lax.dot_general(stack, down, NT, preferred_element_type=jnp.float32)

        @pl.when(step == 0)
        def _():
            total[...] = product

        @pl.when(step > 0)
        def _():
            total[...] += product

    @pl.when(step == steps - 1)
    def _():
        for slot, (total, up) in enumerate(zip(totals, weights(up_refs))):
            wide = expand(total[...], up)
            for k, out in enumerate(outs):
                out[slot * capacity : (slot + 1) * capacity] = wide[
                    k * capacity : (k + 1) * capacity
                ]


def early(inner, first, rest, own_down, own_up, outward, middle, capacity):
    rank, width = own_down.shape
    out_width = own_up.shape[1]
    column = lambda a: pl.BlockSpec((a.shape[0], COLS), lambda c, s: (0, c))
    tail = pl.BlockSpec((rank, out_width), lambda c, s: (0, width // out_width))
    shape = jax.ShapeDtypeStruct((3 * capacity, out_width), jnp.bfloat16)
    return pl.pallas_call(
        functools.partial(early_kernel, capacity),
        grid_spec=pltpu.PrefetchScalarGridSpec(
            num_scalar_prefetch=1,
            grid=(width // COLS,),
            in_specs=[column(a) for a in (*first, *rest, own_down, outward, middle)]
            + [pl.BlockSpec((rank, out_width), lambda c, s: (0, 0)), tail, tail],
            out_specs=[pl.BlockSpec(shape.shape, lambda c, s: (0, 0))] * PLANE,
            scratch_shapes=[pltpu.VMEM((PLANE * capacity, rank), jnp.float32)] * 3,
        ),
        out_shape=[shape] * PLANE,
        compiler_params=params("arbitrary"),
        name="early",
    )(inner, *first, *rest, own_down, outward, middle, own_up, outward, middle)


def late_kernel(capacity, inner_ref, *refs):
    rest, passed = refs[:PLANE], refs[PLANE]
    down_refs, up_refs = refs[PLANE + 1 : PLANE + 3], refs[PLANE + 3 : PLANE + 5]
    outs, total = refs[PLANE + 5 : 3 * PLANE + 5], refs[3 * PLANE + 5]
    step, steps = pl.program_id(0), pl.num_programs(0)
    inner = inner_ref[0] == 1

    def weight(two):
        middle, outward = two
        return jnp.where(inner, middle[...], outward[...])

    stack = jnp.concatenate([r[...] for r in rest] + [passed[...]], axis=0)
    product = lax.dot_general(stack, weight(down_refs), NT, preferred_element_type=jnp.float32)

    @pl.when(step == 0)
    def _():
        total[...] = product

    @pl.when(step > 0)
    def _():
        total[...] += product

    @pl.when(step == steps - 1)
    def _():
        wide = expand(total[...], weight(up_refs))
        for k, out in enumerate(outs):
            out[...] = wide[k * capacity : (k + 1) * capacity]


def late(inner, rest, passed, middle, outward, width, capacity):
    rank = middle.shape[0]
    out_width = middle.shape[1] - width
    last = pl.BlockSpec((capacity, COLS), lambda c, s: (2, c))
    column = lambda a: pl.BlockSpec((a.shape[0], COLS), lambda c, s: (0, c))
    tail = pl.BlockSpec((rank, out_width), lambda c, s: (0, width // out_width))
    shape = jax.ShapeDtypeStruct((capacity, out_width), jnp.bfloat16)
    return pl.pallas_call(
        functools.partial(late_kernel, capacity),
        grid_spec=pltpu.PrefetchScalarGridSpec(
            num_scalar_prefetch=1,
            grid=(width // COLS,),
            in_specs=[last] * PLANE
            + [column(passed), column(middle), column(outward), tail, tail],
            out_specs=[pl.BlockSpec(shape.shape, lambda c, s: (0, 0))] * (2 * PLANE),
            scratch_shapes=[pltpu.VMEM((2 * PLANE * capacity, rank), jnp.float32)],
        ),
        out_shape=[shape] * (2 * PLANE),
        compiler_params=params("arbitrary"),
        name="late",
    )(inner, *rest, passed, middle, outward, middle, outward)


def by_planes(hidden, slot, down, up, capacity):
    devices = lax.axis_size("adapter")
    me = lax.axis_index("adapter")
    plane, place = me // PLANE, me % PLANE
    inner = (plane == 1) | (plane == 2)
    all_devices = range(devices)
    ends = [i for i in all_devices if i // PLANE in (0, 3)]
    middles = [i for i in all_devices if i // PLANE in (1, 2)]
    send = lambda a, pairs: lax.ppermute(a, "adapter", pairs)

    packed = jnp.concatenate([down, up], axis=1)
    outward = send(packed, [(i, i ^ PLANE) for i in all_devices])
    middle = send(packed, [(i, i ^ (3 * PLANE)) for i in middles])

    plane_of, place_of = slot // PLANE, slot % PLANE
    k = place_of ^ place
    distance = jnp.abs(plane_of - plane)
    at_end = (plane_of == 0) | (plane_of == 3)
    kind = jnp.where(
        distance == 0,
        1,
        jnp.where(distance == 2, 3, jnp.where((distance == 3) | at_end, 0, 2)),
    )
    rank = rank_in_slot(slot)
    target = jnp.where(
        kind == 0,
        k * capacity + rank,
        PLANE * capacity + k * 3 * capacity + (kind - 1) * capacity + rank,
    )
    back = jnp.where(
        (kind == 0) & ~inner,
        4 * PLANE * capacity + k * capacity + rank,
        jnp.where(
            kind == 3,
            3 * PLANE * capacity + k * capacity + rank,
            k * 3 * capacity + kind * capacity + rank,
        ),
    )
    outs = pack(target, hidden, capacity)
    first, rest = outs[:PLANE], outs[PLANE:]
    across = [
        [(i, (i // PLANE) * PLANE + ((i % PLANE) ^ k)) for i in all_devices] for k in range(PLANE)
    ]
    first = [first[0]] + [send(first[k], across[k]) for k in range(1, PLANE)]
    rest = [rest[0]] + [send(rest[k], across[k]) for k in range(1, PLANE)]
    outward2 = send(middle, [(i, i ^ PLANE) for i in middles])
    middle2 = send(outward, [(i, i ^ (3 * PLANE)) for i in middles])
    passed = jnp.concatenate(first, axis=0)
    passed, _ = lax.optimization_barrier((passed, outward))
    passed = send(passed, [(i, i ^ PLANE) for i in ends])

    inner_flag = inner.astype(jnp.int32).reshape(1)
    soon = early(inner_flag, first, rest, down, up, outward, middle, capacity)
    soon = [soon[0]] + [send(soon[k], across[k]) for k in range(1, PLANE)]
    outs = late(inner_flag, rest, passed, middle2, outward2, hidden.shape[1], capacity)
    last = [outs[0]] + [send(outs[k], across[k]) for k in range(1, PLANE)]
    far = [
        send(outs[PLANE + k], [(i, (i ^ PLANE) ^ k) for i in middles]) for k in range(PLANE)
    ]
    return back, [*soon, *last, *far]


def by_rows(hidden, slot, down, up, capacity):
    devices = lax.axis_size("adapter")
    target = slot * capacity + rank_in_slot(slot)
    spots = jnp.arange(devices * capacity, dtype=jnp.int32)
    placing = (target[None, :] == spots[:, None]).astype(jnp.bfloat16)
    outgoing = jnp.dot(placing, hidden, preferred_element_type=jnp.float32).astype(jnp.bfloat16)
    outgoing = outgoing.reshape(devices, capacity, hidden.shape[1])
    incoming = lax.all_to_all(outgoing, "adapter", split_axis=0, concat_axis=0, tiled=True)
    rows = incoming.reshape(-1, hidden.shape[1])
    shrunk = lax.dot_general(rows, down, NT, preferred_element_type=jnp.float32)
    wide = expand(shrunk, up)
    returned = lax.all_to_all(
        wide.reshape(devices, capacity, -1), "adapter", split_axis=0, concat_axis=0, tiled=True
    )
    return target, [returned.reshape(devices * capacity, -1)]


def on_device(
    hidden,
    queries,
    base_key_value,
    key_value_cache,
    lengths,
    request_adapter_index,
    adapter_position_map,
    adapter_down_weight,
    adapter_up_weight,
):
    devices = lax.axis_size("adapter")
    capacity = max(2, 2 * hidden.shape[0] // devices)
    slot = slot_lookup(request_adapter_index[:, 0], adapter_position_map)
    deliver = by_planes if devices == 4 * PLANE else by_rows
    target, pieces = deliver(
        hidden, slot, adapter_down_weight[0], adapter_up_weight[0], capacity
    )
    mixed, logs = cached_attention(queries, key_value_cache, lengths)
    return finish(target, base_key_value, queries, mixed, logs, pieces)


def solution(mesh):
    rows = P(("groups", "adapter"), None)
    deep = P(("groups", "adapter"), None, None)
    placed = (
        rows,
        rows,
        rows,
        deep,
        P(("groups", "adapter")),
        rows,
        P("groups"),
        deep,
        deep,
    )
    return jax.shard_map(
        on_device, mesh=mesh, in_specs=placed, out_specs=(rows, rows), check_vma=False
    )
```

```python
import functools

import jax
import jax.numpy as jnp
from jax import lax
from jax.experimental import pallas as pl
from jax.experimental.pallas import tpu as pltpu
from jax.sharding import PartitionSpec as P

QUERY_HEADS = 32
KEY_VALUE_HEADS = 4
HEAD_SIZE = 128
GROUP = QUERY_HEADS // KEY_VALUE_HEADS
SPLIT = KEY_VALUE_HEADS * HEAD_SIZE
PLANE = 4
COLS = 1024
LONG = 20_000_000_000

adapter_scale = 2.0
score_floor = -1e30
score_scale = HEAD_SIZE ** (-0.5)

NT = (((1,), (1,)), ((), ()))


def slot_lookup(request_adapter, adapter_position_map):
    adapter_index = jnp.arange(adapter_position_map.shape[0], dtype=jnp.int32)
    matches = request_adapter[:, None] == adapter_index[None, :]
    return jnp.sum(jnp.where(matches, adapter_position_map[None, :], 0), axis=1)


def rank_in_slot(slot):
    order = jnp.arange(slot.shape[0], dtype=jnp.int32)
    same = slot[:, None] == slot[None, :]
    before = order[None, :] < order[:, None]
    return jnp.sum((same & before).astype(jnp.int32), axis=1)


VMEM = pl.BlockSpec(memory_space=pltpu.VMEM)
SMEM = pl.BlockSpec(memory_space=pltpu.SMEM)
HBM = pl.BlockSpec(memory_space=pltpu.HBM)


def options(name, cost=None):
    chosen = dict(
        name=name, compiler_params=pltpu.CompilerParams(vmem_limit_bytes=12 * 1024 * 1024)
    )
    if cost is not None:
        chosen["cost_estimate"] = pl.CostEstimate(
            flops=1000, bytes_accessed=cost, transcendentals=0
        )
    return chosen


def chunks(width):
    return [slice(c, c + COLS) for c in range(0, width, COLS)]


def cached_kernel(step, length_ref, q_ref, cache_ref, mixed_ref, log_ref):
    total, context = cache_ref.shape[0], cache_ref.shape[1]
    keys = step * context
    owner_q = lax.rem(lax.broadcasted_iota(jnp.int32, (GROUP * step, keys), 0), step)
    column = lax.broadcasted_iota(jnp.int32, (GROUP * step, keys), 1)
    owner_k, position = column // context, lax.rem(column, context)
    lane = lax.broadcasted_iota(jnp.int32, (step, HEAD_SIZE), 1)

    def requests(i, carry):
        rows = pl.ds(pl.multiple_of(i * step, step), step)
        lengths = jnp.concatenate([length_ref[rows, :]] * GROUP, axis=0)
        included = (owner_q == owner_k) & (position < lengths)
        logs = jnp.zeros((step, HEAD_SIZE), jnp.float32)
        for head in range(KEY_VALUE_HEADS):
            first = head * GROUP
            q = jnp.concatenate(
                [
                    q_ref[rows, (first + g) * HEAD_SIZE : (first + g + 1) * HEAD_SIZE]
                    for g in range(GROUP)
                ],
                axis=0,
            )
            k = cache_ref[rows, :, head * HEAD_SIZE : (head + 1) * HEAD_SIZE]
            v = cache_ref[rows, :, SPLIT + head * HEAD_SIZE : SPLIT + (head + 1) * HEAD_SIZE]
            k, v = k.reshape(keys, HEAD_SIZE), v.reshape(keys, HEAD_SIZE)
            score = lax.dot_general(q, k, NT, preferred_element_type=jnp.float32) * score_scale
            score = jnp.where(included, score, score_floor)
            peak = jnp.max(score, axis=1, keepdims=True)
            weight = jnp.exp(score - peak)
            denominator = jnp.sum(weight, axis=1, keepdims=True)
            mixed = jnp.dot(weight.astype(jnp.bfloat16), v, preferred_element_type=jnp.float32)
            mixed = mixed / denominator
            log = peak + jnp.log(denominator)
            for g in range(GROUP):
                part = slice(g * step, (g + 1) * step)
                mixed_ref[rows, (first + g) * HEAD_SIZE : (first + g + 1) * HEAD_SIZE] = mixed[
                    part
                ]
                logs = jnp.where(lane == first + g, log[part], logs)
        log_ref[rows, :] = logs
        return carry

    lax.fori_loop(0, total // step, requests, 0)


def cached_attention(queries, cache, lengths):
    rows = cache.shape[0]
    return pl.pallas_call(
        functools.partial(cached_kernel, 16),
        in_specs=[VMEM] * 3,
        out_specs=[VMEM] * 2,
        out_shape=[
            jax.ShapeDtypeStruct(queries.shape, jnp.float32),
            jax.ShapeDtypeStruct((rows, HEAD_SIZE), jnp.float32),
        ],
        **options("cached", LONG),
    )(lengths.reshape(rows, 1), queries, cache)


def finish_kernel(count, target_ref, base_ref, q_ref, mixed_ref, log_ref, *refs):
    pieces, refs = refs[:count], refs[count:]
    attention_hbm, written_hbm, attention_ref, written_ref, stack_ref, sems, piece_sems = refs
    rows = base_ref.shape[0]
    total = stack_ref.shape[0]
    arrivals, start = [], 0
    for i, piece in enumerate(pieces):
        spot = stack_ref.at[start : start + piece.shape[0]]
        arrivals.append(pltpu.make_async_copy(piece, spot, piece_sems.at[i]))
        arrivals[-1].start()
        start += piece.shape[0]
    spots = lax.broadcasted_iota(jnp.int32, (rows, total), 1)
    place = (spots == target_ref[...]).astype(jnp.float32).astype(jnp.bfloat16)
    for arrival in arrivals:
        arrival.wait()
    delta = jnp.dot(place, stack_ref[...], preferred_element_type=jnp.float32)
    written_ref[...] = (base_ref[...].astype(jnp.float32) + delta).astype(jnp.bfloat16)
    copies = [pltpu.make_async_copy(written_ref, written_hbm, sems.at[KEY_VALUE_HEADS])]
    copies[0].start()
    lane = lax.broadcasted_iota(jnp.int32, (rows, HEAD_SIZE), 1)
    logs = log_ref[...]
    for head in range(KEY_VALUE_HEADS):
        own = slice(head * HEAD_SIZE, (head + 1) * HEAD_SIZE)
        new_key = written_ref[:, own].astype(jnp.float32)
        own = slice(SPLIT + head * HEAD_SIZE, SPLIT + (head + 1) * HEAD_SIZE)
        new_value = written_ref[:, own].astype(jnp.float32)
        for i in range(head * GROUP, (head + 1) * GROUP):
            part = slice(i * HEAD_SIZE, (i + 1) * HEAD_SIZE)
            query = q_ref[:, part].astype(jnp.float32)
            score = jnp.sum(query * new_key, axis=1, keepdims=True) * score_scale
            log = jnp.sum(jnp.where(lane == i, logs, 0.0), axis=1, keepdims=True)
            share = 1.0 / (1.0 + jnp.exp(score - log))
            out = new_value + share * (mixed_ref[:, part] - new_value)
            attention_ref[:, part] = out.astype(jnp.bfloat16)
        wide = slice(head * GROUP * HEAD_SIZE, (head + 1) * GROUP * HEAD_SIZE)
        copies.append(
            pltpu.make_async_copy(
                attention_ref.at[:, wide], attention_hbm.at[:, wide], sems.at[head]
            )
        )
        copies[-1].start()
    for copy in copies:
        copy.wait()


def finish(target, base, queries, mixed, logs, pieces):
    rows = base.shape[0]
    return pl.pallas_call(
        functools.partial(finish_kernel, len(pieces)),
        in_specs=[VMEM] * 5 + [HBM] * len(pieces),
        out_specs=[HBM] * 2,
        out_shape=[
            jax.ShapeDtypeStruct(queries.shape, jnp.bfloat16),
            jax.ShapeDtypeStruct(base.shape, jnp.bfloat16),
        ],
        scratch_shapes=[
            pltpu.VMEM(queries.shape, jnp.bfloat16),
            pltpu.VMEM(base.shape, jnp.bfloat16),
            pltpu.VMEM((sum(piece.shape[0] for piece in pieces), base.shape[1]), jnp.bfloat16),
            pltpu.SemaphoreType.DMA((KEY_VALUE_HEADS + 1,)),
            pltpu.SemaphoreType.DMA((len(pieces),)),
        ],
        **options("finish"),
    )(target.reshape(rows, 1), base, queries, mixed, logs, *pieces)


def pack_kernel(target_ref, hidden_ref, *outs):
    height = outs[0].shape[0]
    spots = height * len(outs)
    spot = lax.broadcasted_iota(jnp.int32, (spots, hidden_ref.shape[0]), 0)
    place = (spot == target_ref[...]).astype(jnp.float32).astype(jnp.bfloat16)
    for part in chunks(hidden_ref.shape[1]):
        packed = jnp.dot(place, hidden_ref[:, part], preferred_element_type=jnp.float32)
        packed = packed.astype(jnp.bfloat16)
        for k, out in enumerate(outs):
            out[:, part] = packed[k * height : (k + 1) * height]


def pack(target, hidden, height, cost):
    rows, width = hidden.shape
    return pl.pallas_call(
        pack_kernel,
        in_specs=[VMEM] * 2,
        out_specs=[VMEM] * PLANE,
        out_shape=[jax.ShapeDtypeStruct((height, width), jnp.bfloat16)] * PLANE,
        **options("pack", cost),
    )(target.reshape(1, rows), hidden)


def expand(total, up):
    shrunk = total.astype(jnp.bfloat16)
    wide = jnp.dot(shrunk, up, preferred_element_type=jnp.float32)
    return (adapter_scale * wide).astype(jnp.bfloat16)


def shrink(row_parts, downs):
    total = None
    for part in chunks(row_parts[0].shape[1]):
        rows = jnp.concatenate([ref[:, part] for ref in row_parts], axis=0)
        down = jnp.concatenate([ref[:, part] for ref in downs], axis=0)
        product = lax.dot_general(rows, down, NT, preferred_element_type=jnp.float32)
        total = product if total is None else total + product
    return total


def both_slots(capacity, total, ups, outs, first=0):
    for slot, up in enumerate(ups):
        rank = up.shape[0]
        lanes = slice(slot * rank, (slot + 1) * rank)
        starts = [(2 * k + slot) * capacity for k in range(PLANE)]
        sums = jnp.concatenate([total[i : i + capacity, lanes] for i in starts], axis=0)
        wide = expand(sums, up)
        start = (first + slot) * capacity
        for k, out in enumerate(outs):
            out[start : start + capacity] = wide[k * capacity : (k + 1) * capacity]


def join_kernel(down_hbm, up_hbm, out_ref, sems):
    width = down_hbm.shape[1]
    down = pltpu.make_async_copy(down_hbm, out_ref.at[:, :width], sems.at[0])
    up = pltpu.make_async_copy(up_hbm, out_ref.at[:, width:], sems.at[1])
    down.start()
    up.start()
    down.wait()
    up.wait()


def join(down, up):
    return pl.pallas_call(
        join_kernel,
        in_specs=[HBM] * 2,
        out_specs=VMEM,
        out_shape=jax.ShapeDtypeStruct((down.shape[0], down.shape[1] + up.shape[1]), down.dtype),
        scratch_shapes=[pltpu.SemaphoreType.DMA((2,))],
        **options("join"),
    )(down, up)


def early_kernel(capacity, *refs):
    rows, (outward, own), out = refs[:PLANE], refs[PLANE : PLANE + 2], refs[PLANE + 2]
    width = rows[0].shape[1]
    total = shrink(rows, [outward, own])
    outs = [out.at[2 * k * capacity : 2 * (k + 1) * capacity] for k in range(PLANE)]
    both_slots(capacity, total, (outward[:, width:], own[:, width:]), outs)


def early(rows, outward, own, capacity):
    out_width = own.shape[1] - rows[0].shape[1]
    return pl.pallas_call(
        functools.partial(early_kernel, capacity),
        in_specs=[VMEM] * (PLANE + 2),
        out_specs=VMEM,
        out_shape=jax.ShapeDtypeStruct((2 * PLANE * capacity, out_width), jnp.bfloat16),
        **options("early"),
    )(*rows, outward, own)


def late_kernel(capacity, where_ref, soon_ref, *refs):
    rows, refs = refs[:PLANE], refs[PLANE:]
    outward, middle, middle2, swapped = refs[:4]
    outs, fars = refs[4 : 4 + PLANE], refs[4 + PLANE :]
    width = rows[0].shape[1]
    for k, out in enumerate(outs):
        out[: 2 * capacity] = soon_ref[2 * k * capacity : 2 * (k + 1) * capacity]

    @pl.when(where_ref[0] == 1)
    def _():
        total = shrink([*rows, swapped], [middle, middle2])
        both_slots(capacity, total, (middle[:, width:], middle2[:, width:]), outs, 2)
        wide = expand(total[2 * PLANE * capacity :, middle.shape[0] :], middle2[:, width:])
        for k, far in enumerate(fars):
            far[...] = wide[k * capacity : (k + 1) * capacity]

    @pl.when(where_ref[0] == 0)
    def _():
        total = shrink(rows, [outward, swapped])
        both_slots(capacity, total, (outward[:, width:], swapped[:, width:]), outs, 2)
        for far in fars:
            far[...] = jnp.zeros(far.shape, far.dtype)


def late(where, soon, rows, weights, capacity):
    out_width = weights[0].shape[1] - rows[0].shape[1]
    near = jax.ShapeDtypeStruct((4 * capacity, out_width), jnp.bfloat16)
    far = jax.ShapeDtypeStruct((capacity, out_width), jnp.bfloat16)
    return pl.pallas_call(
        functools.partial(late_kernel, capacity),
        in_specs=[SMEM] + [VMEM] * (PLANE + 5),
        out_specs=[VMEM] * (2 * PLANE),
        out_shape=[near] * PLANE + [far] * PLANE,
        **options("late"),
    )(where, soon, *rows, *weights)


def choose_kernel(where_ref, weights_ref, *refs):
    rows, out = refs[:PLANE], refs[PLANE]
    capacity, width = out.shape[0] // PLANE, rows[0].shape[1]

    @pl.when(where_ref[0] == 1)
    def _():
        out[...] = weights_ref[...]

    @pl.when(where_ref[0] == 0)
    def _():
        for k, ref in enumerate(rows):
            out[k * capacity : (k + 1) * capacity, :width] = ref[:capacity]
        out[:, width:] = jnp.zeros((out.shape[0], out.shape[1] - width), out.dtype)


def choose(where, weights, rows):
    return pl.pallas_call(
        choose_kernel,
        in_specs=[SMEM] + [VMEM] * (1 + PLANE),
        out_specs=VMEM,
        out_shape=jax.ShapeDtypeStruct(weights.shape, weights.dtype),
        **options("choose"),
    )(where, weights, *rows)


def by_planes(hidden, slot, down, up, capacity, meanwhile):
    devices = lax.axis_size("adapter")
    me = lax.axis_index("adapter")
    plane, place = me // PLANE, me % PLANE
    inner = (plane == 1) | (plane == 2)
    where = inner.astype(jnp.int32).reshape(1)
    all_devices = range(devices)
    middles = [i for i in all_devices if i // PLANE in (1, 2)]
    across = [
        [(i, (i // PLANE) * PLANE + ((i % PLANE) ^ k)) for i in all_devices] for k in range(PLANE)
    ]
    to_outward = [(i, i ^ PLANE) for i in all_devices]
    to_middle = [(i, i ^ (3 * PLANE)) for i in middles]
    send = lambda a, pairs: lax.ppermute(a, "adapter", pairs)
    exchange = lambda parts: [parts[0]] + [send(parts[k], across[k]) for k in range(1, PLANE)]

    plane_of, place_of = slot // PLANE, slot % PLANE
    distance = jnp.abs(plane_of - plane)
    at_end = (plane_of == 0) | (plane_of == 3)
    kind = jnp.where(
        distance == 0,
        1,
        jnp.where(distance == 2, 3, jnp.where((distance == 3) | at_end, 0, 2)),
    )
    rank = rank_in_slot(slot)
    k = place_of ^ place
    spot = (k * 2 + kind % 2) * capacity + rank
    spots = 2 * PLANE * capacity
    back = jnp.where(
        (kind == 0) & ~inner,
        2 * spots + k * capacity + rank,
        (k * 4 + kind) * capacity + rank,
    )

    weights = join(down, up)
    outward, middle = send(weights, to_outward), send(weights, to_middle)
    near = exchange(pack(jnp.where(kind < 2, spot, -1), hidden, 2 * capacity, None))
    away = pack(jnp.where(kind < 2, -1, spot), hidden, 2 * capacity, LONG)
    near, away, outward, middle = lax.optimization_barrier((near, away, outward, middle))
    middle2 = send(outward, to_middle)
    swapped = send(choose(where, middle, near), to_outward)
    away = exchange(away)

    done = meanwhile()
    near, done = lax.optimization_barrier((near, done))
    soon = early(near, outward, weights, capacity)
    where, done, soon = lax.optimization_barrier((where, done, soon))
    outs = late(where, soon, away, [outward, middle, middle2, swapped], capacity)
    last = exchange(outs[:PLANE])
    far = [send(outs[PLANE + k], [(i, (i ^ PLANE) ^ k) for i in middles]) for k in range(PLANE)]
    return back, [*last, *far], done


def by_rows(hidden, slot, down, up, capacity, meanwhile):
    devices = lax.axis_size("adapter")
    target = slot * capacity + rank_in_slot(slot)
    spots = jnp.arange(devices * capacity, dtype=jnp.int32)
    placing = (target[None, :] == spots[:, None]).astype(jnp.bfloat16)
    outgoing = jnp.dot(placing, hidden, preferred_element_type=jnp.float32).astype(jnp.bfloat16)
    outgoing = outgoing.reshape(devices, capacity, hidden.shape[1])
    incoming = lax.all_to_all(outgoing, "adapter", split_axis=0, concat_axis=0, tiled=True)
    rows = incoming.reshape(-1, hidden.shape[1])
    shrunk = lax.dot_general(rows, down, NT, preferred_element_type=jnp.float32)
    wide = expand(shrunk, up)
    returned = lax.all_to_all(
        wide.reshape(devices, capacity, -1), "adapter", split_axis=0, concat_axis=0, tiled=True
    )
    return target, [returned.reshape(devices * capacity, -1)], meanwhile()


def on_device(
    hidden,
    queries,
    base_key_value,
    key_value_cache,
    lengths,
    request_adapter_index,
    adapter_position_map,
    adapter_down_weight,
    adapter_up_weight,
):
    devices = lax.axis_size("adapter")
    capacity = max(2, 2 * hidden.shape[0] // devices)
    slot = slot_lookup(request_adapter_index[:, 0], adapter_position_map)
    deliver = by_planes if devices == 4 * PLANE else by_rows
    meanwhile = lambda: cached_attention(queries, key_value_cache, lengths)
    target, pieces, (mixed, logs) = deliver(
        hidden, slot, adapter_down_weight[0], adapter_up_weight[0], capacity, meanwhile
    )
    return finish(target, base_key_value, queries, mixed, logs, pieces)


def solution(mesh):
    rows = P(("groups", "adapter"), None)
    deep = P(("groups", "adapter"), None, None)
    placed = (
        rows,
        rows,
        rows,
        deep,
        P(("groups", "adapter")),
        rows,
        P("groups"),
        deep,
        deep,
    )
    return jax.shard_map(
        on_device, mesh=mesh, in_specs=placed, out_specs=(rows, rows), check_vma=False
    )
```

```python
import functools

import jax
import jax.numpy as jnp
from jax import lax
from jax.experimental import pallas as pl
from jax.experimental.pallas import tpu as pltpu
from jax.sharding import PartitionSpec as P

QUERY_HEADS = 32
KEY_VALUE_HEADS = 4
HEAD_SIZE = 128
GROUP = QUERY_HEADS // KEY_VALUE_HEADS
SPLIT = KEY_VALUE_HEADS * HEAD_SIZE
PLANE = 4
COLS = 2048
LONG = 20_000_000_000

adapter_scale = 2.0
score_floor = -1e30
score_scale = HEAD_SIZE ** (-0.5)

NT = (((1,), (1,)), ((), ()))


def slot_lookup(request_adapter, adapter_position_map):
    adapter_index = jnp.arange(adapter_position_map.shape[0], dtype=jnp.int32)
    matches = request_adapter[:, None] == adapter_index[None, :]
    return jnp.sum(jnp.where(matches, adapter_position_map[None, :], 0), axis=1)


def rank_in_slot(slot):
    order = jnp.arange(slot.shape[0], dtype=jnp.int32)
    same = slot[:, None] == slot[None, :]
    before = order[None, :] < order[:, None]
    return jnp.sum((same & before).astype(jnp.int32), axis=1)


VMEM = pl.BlockSpec(memory_space=pltpu.VMEM)
SMEM = pl.BlockSpec(memory_space=pltpu.SMEM)
HBM = pl.BlockSpec(memory_space=pltpu.HBM)


def options(name, cost=None, mebibytes=12):
    chosen = dict(
        name=name,
        compiler_params=pltpu.CompilerParams(vmem_limit_bytes=mebibytes * 1024 * 1024),
    )
    if cost is not None:
        chosen["cost_estimate"] = pl.CostEstimate(
            flops=1000, bytes_accessed=cost, transcendentals=0
        )
    return chosen


def chunks(width):
    return [slice(c, c + COLS) for c in range(0, width, COLS)]


def cached_kernel(step, length_ref, q_ref, cache_ref, mixed_ref, log_ref):
    total, context = cache_ref.shape[0], cache_ref.shape[1]
    keys = step * context
    owner_q = lax.rem(lax.broadcasted_iota(jnp.int32, (GROUP * step, keys), 0), step)
    column = lax.broadcasted_iota(jnp.int32, (GROUP * step, keys), 1)
    owner_k, position = column // context, lax.rem(column, context)
    lane = lax.broadcasted_iota(jnp.int32, (step, HEAD_SIZE), 1)

    def requests(i, carry):
        rows = pl.ds(pl.multiple_of(i * step, step), step)
        lengths = jnp.concatenate([length_ref[rows, :]] * GROUP, axis=0)
        included = (owner_q == owner_k) & (position < lengths)
        logs = jnp.zeros((step, HEAD_SIZE), jnp.float32)
        for head in range(KEY_VALUE_HEADS):
            first = head * GROUP
            q = jnp.concatenate(
                [
                    q_ref[rows, (first + g) * HEAD_SIZE : (first + g + 1) * HEAD_SIZE]
                    for g in range(GROUP)
                ],
                axis=0,
            )
            k = cache_ref[rows, :, head * HEAD_SIZE : (head + 1) * HEAD_SIZE]
            v = cache_ref[rows, :, SPLIT + head * HEAD_SIZE : SPLIT + (head + 1) * HEAD_SIZE]
            k, v = k.reshape(keys, HEAD_SIZE), v.reshape(keys, HEAD_SIZE)
            score = lax.dot_general(q, k, NT, preferred_element_type=jnp.float32) * score_scale
            score = jnp.where(included, score, score_floor)
            peak = jnp.max(score, axis=1, keepdims=True)
            weight = jnp.exp(score - peak)
            denominator = jnp.sum(weight, axis=1, keepdims=True)
            mixed = jnp.dot(weight.astype(jnp.bfloat16), v, preferred_element_type=jnp.float32)
            mixed = (mixed / denominator).astype(jnp.bfloat16)
            log = peak + jnp.log(denominator)
            for g in range(GROUP):
                part = slice(g * step, (g + 1) * step)
                mixed_ref[rows, (first + g) * HEAD_SIZE : (first + g + 1) * HEAD_SIZE] = mixed[
                    part
                ]
                logs = jnp.where(lane == first + g, log[part], logs)
        log_ref[rows, :] = logs
        return carry

    lax.fori_loop(0, total // step, requests, 0)


def cached_attention(queries, cache, lengths):
    rows = cache.shape[0]
    return pl.pallas_call(
        functools.partial(cached_kernel, 16),
        in_specs=[VMEM] * 3,
        out_specs=[VMEM] * 2,
        out_shape=[
            jax.ShapeDtypeStruct(queries.shape, jnp.bfloat16),
            jax.ShapeDtypeStruct((rows, HEAD_SIZE), jnp.float32),
        ],
        **options("cached", LONG),
    )(lengths.reshape(rows, 1), queries, cache)


def finish_kernel(count, target_ref, base_ref, q_ref, log_ref, mixed_hbm, *refs):
    pieces, refs = refs[:count], refs[count:]
    attention_hbm, written_hbm, attention_ref, written_ref, stack_ref, mixed_ref = refs[:6]
    sems, piece_sems, mixed_sems = refs[6:]
    rows = base_ref.shape[0]
    total = stack_ref.shape[0]
    arrivals, start = [], 0
    for i, piece in enumerate(pieces):
        spot = stack_ref.at[start : start + piece.shape[0]]
        arrivals.append(pltpu.make_async_copy(piece, spot, piece_sems.at[i]))
        arrivals[-1].start()
        start += piece.shape[0]
    spots = lax.broadcasted_iota(jnp.int32, (rows, total), 1)
    place = (spots == target_ref[...]).astype(jnp.float32).astype(jnp.bfloat16)
    mixes = []
    for head in range(KEY_VALUE_HEADS):
        wide = slice(head * GROUP * HEAD_SIZE, (head + 1) * GROUP * HEAD_SIZE)
        mixes.append(
            pltpu.make_async_copy(
                mixed_hbm.at[:, wide], mixed_ref.at[:, wide], mixed_sems.at[head]
            )
        )
        mixes[-1].start()
    for arrival in arrivals:
        arrival.wait()
    delta = jnp.dot(place, stack_ref[...], preferred_element_type=jnp.float32)
    written_ref[...] = (base_ref[...].astype(jnp.float32) + delta).astype(jnp.bfloat16)
    copies = [pltpu.make_async_copy(written_ref, written_hbm, sems.at[KEY_VALUE_HEADS])]
    copies[0].start()
    lane = lax.broadcasted_iota(jnp.int32, (rows, HEAD_SIZE), 1)
    logs = log_ref[...]
    for head in range(KEY_VALUE_HEADS):
        own = slice(head * HEAD_SIZE, (head + 1) * HEAD_SIZE)
        new_key = written_ref[:, own].astype(jnp.float32)
        own = slice(SPLIT + head * HEAD_SIZE, SPLIT + (head + 1) * HEAD_SIZE)
        new_value = written_ref[:, own].astype(jnp.float32)
        mixes[head].wait()
        for i in range(head * GROUP, (head + 1) * GROUP):
            part = slice(i * HEAD_SIZE, (i + 1) * HEAD_SIZE)
            query = q_ref[:, part].astype(jnp.float32)
            score = jnp.sum(query * new_key, axis=1, keepdims=True) * score_scale
            log = jnp.sum(jnp.where(lane == i, logs, 0.0), axis=1, keepdims=True)
            share = 1.0 / (1.0 + jnp.exp(score - log))
            out = new_value + share * (mixed_ref[:, part].astype(jnp.float32) - new_value)
            attention_ref[:, part] = out.astype(jnp.bfloat16)
        wide = slice(head * GROUP * HEAD_SIZE, (head + 1) * GROUP * HEAD_SIZE)
        copies.append(
            pltpu.make_async_copy(
                attention_ref.at[:, wide], attention_hbm.at[:, wide], sems.at[head]
            )
        )
        copies[-1].start()
    for copy in copies:
        copy.wait()


def finish(target, base, queries, mixed, logs, pieces):
    rows = base.shape[0]
    return pl.pallas_call(
        functools.partial(finish_kernel, len(pieces)),
        in_specs=[VMEM] * 4 + [HBM] * (1 + len(pieces)),
        out_specs=[HBM] * 2,
        out_shape=[
            jax.ShapeDtypeStruct(queries.shape, jnp.bfloat16),
            jax.ShapeDtypeStruct(base.shape, jnp.bfloat16),
        ],
        scratch_shapes=[
            pltpu.VMEM(queries.shape, jnp.bfloat16),
            pltpu.VMEM(base.shape, jnp.bfloat16),
            pltpu.VMEM((sum(piece.shape[0] for piece in pieces), base.shape[1]), jnp.bfloat16),
            pltpu.VMEM(mixed.shape, mixed.dtype),
            pltpu.SemaphoreType.DMA((KEY_VALUE_HEADS + 1,)),
            pltpu.SemaphoreType.DMA((len(pieces),)),
            pltpu.SemaphoreType.DMA((KEY_VALUE_HEADS,)),
        ],
        **options("finish", 1000),
    )(target.reshape(rows, 1), base, queries, logs, mixed, *pieces)


def pack_kernel(target_ref, hidden_hbm, *refs):
    outs, (hidden_ref, packed_ref, hidden_sems, sems) = refs[:-4], refs[-4:]
    spots = packed_ref.shape[0]
    parts = chunks(hidden_ref.shape[1])
    fetches, stores = [], []
    for i, part in enumerate(parts):
        fetches.append(
            pltpu.make_async_copy(
                hidden_hbm.at[:, part], hidden_ref.at[:, part], hidden_sems.at[i]
            )
        )
        fetches[-1].start()
    spot = lax.broadcasted_iota(jnp.int32, (spots, hidden_ref.shape[0]), 0)
    place = (spot == target_ref[...]).astype(jnp.float32).astype(jnp.bfloat16)
    for i, part in enumerate(parts):
        fetches[i].wait()
        packed = jnp.dot(place, hidden_ref[:, part], preferred_element_type=jnp.float32)
        packed_ref[:, part] = packed.astype(jnp.bfloat16)
        start = 0
        for j, out in enumerate(outs):
            own = packed_ref.at[start : start + out.shape[0], part]
            stores.append(pltpu.make_async_copy(own, out.at[:, part], sems.at[i, j]))
            stores[-1].start()
            start += out.shape[0]
    for store in stores:
        store.wait()


def pack(target, hidden, heights, cost):
    rows, width = hidden.shape
    steps = len(chunks(width))
    return pl.pallas_call(
        pack_kernel,
        in_specs=[VMEM, HBM],
        out_specs=[HBM] * len(heights),
        out_shape=[jax.ShapeDtypeStruct((height, width), jnp.bfloat16) for height in heights],
        scratch_shapes=[
            pltpu.VMEM(hidden.shape, jnp.bfloat16),
            pltpu.VMEM((sum(heights), width), jnp.bfloat16),
            pltpu.SemaphoreType.DMA((steps,)),
            pltpu.SemaphoreType.DMA((steps, len(heights))),
        ],
        **options("pack", cost, 60),
    )(target.reshape(1, rows), hidden)


def pack_first_kernel(target_ref, hidden_ref, *outs):
    height = outs[0].shape[0]
    spot = lax.broadcasted_iota(jnp.int32, (height * len(outs), hidden_ref.shape[0]), 0)
    place = (spot == target_ref[...]).astype(jnp.float32).astype(jnp.bfloat16)
    for part in chunks(hidden_ref.shape[1]):
        packed = jnp.dot(place, hidden_ref[:, part], preferred_element_type=jnp.float32)
        packed = packed.astype(jnp.bfloat16)
        for i, out in enumerate(outs):
            out[:, part] = packed[i * height : (i + 1) * height]


def pack_first(target, hidden, height, count):
    rows, width = hidden.shape
    return pl.pallas_call(
        pack_first_kernel,
        in_specs=[VMEM] * 2,
        out_specs=[VMEM] * count,
        out_shape=[jax.ShapeDtypeStruct((height, width), jnp.bfloat16)] * count,
        **options("first"),
    )(target.reshape(1, rows), hidden)


def expand(total, up):
    shrunk = total.astype(jnp.bfloat16)
    wide = jnp.dot(shrunk, up, preferred_element_type=jnp.float32)
    return (adapter_scale * wide).astype(jnp.bfloat16)


def shrink(row_parts, downs):
    total = None
    for part in chunks(row_parts[0].shape[1]):
        rows = jnp.concatenate([ref[:, part] for ref in row_parts], axis=0)
        down = jnp.concatenate([ref[:, part] for ref in downs], axis=0)
        product = lax.dot_general(rows, down, NT, preferred_element_type=jnp.float32)
        total = product if total is None else total + product
    return total


def put(out, dest, slots, slot, rows):
    height = rows.shape[0]
    start = pl.multiple_of((dest * slots + slot) * height, height)
    out[pl.ds(start, height), :] = rows


def join_kernel(down_hbm, up_hbm, out_ref, sems):
    width = down_hbm.shape[1]
    down = pltpu.make_async_copy(down_hbm, out_ref.at[:, :width], sems.at[0])
    up = pltpu.make_async_copy(up_hbm, out_ref.at[:, width:], sems.at[1])
    down.start()
    up.start()
    down.wait()
    up.wait()


def join(down, up):
    return pl.pallas_call(
        join_kernel,
        in_specs=[HBM] * 2,
        out_specs=VMEM,
        out_shape=jax.ShapeDtypeStruct((down.shape[0], down.shape[1] + up.shape[1]), down.dtype),
        scratch_shapes=[pltpu.SemaphoreType.DMA((2,))],
        **options("join", 1000, 60),
    )(down, up)


def early_kernel(capacity, where_ref, *refs):
    rows, (outward, middle, own, *outs) = refs[: 3 * PLANE], refs[3 * PLANE :]
    width, rank = rows[0].shape[1], own.shape[0]

    def run(weights):
        total = shrink(rows, weights)
        for slot, weight in enumerate(weights):
            start = slot * PLANE * capacity
            sums = total[start : start + PLANE * capacity, slot * rank : (slot + 1) * rank]
            wide = expand(sums, weight[:, width:])
            for k, out in enumerate(outs):
                out[slot * capacity : (slot + 1) * capacity] = wide[
                    k * capacity : (k + 1) * capacity
                ]

    pl.when(where_ref[0] == 1)(lambda: run([outward, own, middle]))
    pl.when(where_ref[0] == 0)(lambda: run([outward, own, outward]))


def early(where, rows, outward, middle, own, capacity):
    out_width = own.shape[1] - rows[0].shape[1]
    return pl.pallas_call(
        functools.partial(early_kernel, capacity),
        in_specs=[SMEM] + [VMEM] * (3 * PLANE + 3),
        out_specs=[VMEM] * PLANE,
        out_shape=[jax.ShapeDtypeStruct((3 * capacity, out_width), jnp.bfloat16)] * PLANE,
        **options("early", LONG),
    )(where, *rows, outward, middle, own)


def late_kernel(capacity, where_ref, *refs):
    rows, (middle2, swapped, out) = refs[:PLANE], refs[PLANE:]
    width = rows[0].shape[1]
    place, here, there = where_ref[1], where_ref[2], where_ref[3]

    def spread(first, wide):
        for k in range(PLANE):
            put(out, first + (place ^ k), 1, 0, wide[k * capacity : (k + 1) * capacity])

    @pl.when(where_ref[0] == 1)
    def _():
        total = shrink([*rows, swapped], [middle2])
        wide = expand(total, middle2[:, width:])
        spread(here, wide)
        spread(there, wide[PLANE * capacity :])

    @pl.when(where_ref[0] == 0)
    def _():
        wide = expand(shrink(rows, [swapped]), swapped[:, width:])
        spread(here, wide)
        spread(there, jnp.zeros(wide.shape, wide.dtype))


def late(where, rows, middle2, swapped, capacity):
    out_width = swapped.shape[1] - rows[0].shape[1]
    return pl.pallas_call(
        functools.partial(late_kernel, capacity),
        in_specs=[SMEM] + [VMEM] * (PLANE + 2),
        out_specs=VMEM,
        out_shape=jax.ShapeDtypeStruct((2 * PLANE * capacity, out_width), jnp.bfloat16),
        **options("late"),
    )(where, *rows, middle2, swapped)


def choose_kernel(where_ref, weights_hbm, *refs):
    rows, (out_hbm, stack_ref, sems) = refs[:PLANE], refs[PLANE:]
    capacity, width = stack_ref.shape[0] // PLANE, stack_ref.shape[1]

    @pl.when(where_ref[0] == 0)
    def _():
        copies = []
        for k, ref in enumerate(rows):
            for i, part in enumerate(chunks(width)):
                here = stack_ref.at[k * capacity : (k + 1) * capacity, part]
                there = out_hbm.at[k * capacity : (k + 1) * capacity, part]
                fetch = pltpu.make_async_copy(ref.at[:, part], here, sems.at[0, k, i])
                copies.append((fetch, pltpu.make_async_copy(here, there, sems.at[1, k, i])))
                fetch.start()
        for fetch, store in copies:
            fetch.wait()
            store.start()
        for _, store in copies:
            store.wait()


def choose(where, weights, rows):
    height, width = rows[0].shape
    return pl.pallas_call(
        choose_kernel,
        in_specs=[SMEM] + [HBM] * (1 + PLANE),
        out_specs=HBM,
        out_shape=jax.ShapeDtypeStruct(weights.shape, weights.dtype),
        scratch_shapes=[
            pltpu.VMEM((height * PLANE, width), weights.dtype),
            pltpu.SemaphoreType.DMA((2, PLANE, len(chunks(width)))),
        ],
        input_output_aliases={1: 0},
        **options("choose", 1000, 60),
    )(where, weights, *rows)


def by_planes(hidden, slot, down, up, capacity, meanwhile):
    devices = lax.axis_size("adapter")
    me = lax.axis_index("adapter")
    plane, place = me // PLANE, me % PLANE
    inner = (plane == 1) | (plane == 2)
    here = plane % 2 * PLANE
    where = jnp.stack([inner.astype(jnp.int32), place, here, PLANE - here]).astype(jnp.int32)
    all_devices = range(devices)
    middles = [i for i in all_devices if i // PLANE in (1, 2)]
    across = [
        [(i, (i // PLANE) * PLANE + ((i % PLANE) ^ k)) for i in all_devices] for k in range(PLANE)
    ]
    to_outward = [(i, i ^ PLANE) for i in all_devices]
    to_middle = [(i, i ^ (3 * PLANE)) for i in middles]
    send = lambda a, pairs: lax.ppermute(a, "adapter", pairs)

    def gather(rows, size):
        parts = rows.reshape(size, -1, rows.shape[1])
        groups = [list(range(i, i + size)) for i in range(0, devices, size)]
        parts = lax.all_to_all(parts, "adapter", 0, 0, axis_index_groups=groups, tiled=True)
        return parts.reshape(rows.shape)

    exchange = lambda parts: [parts[0]] + [send(parts[k], across[k]) for k in range(1, PLANE)]

    plane_of, place_of = slot // PLANE, slot % PLANE
    distance = jnp.abs(plane_of - plane)
    at_end = (plane_of == 0) | (plane_of == 3)
    kind = jnp.where(
        distance == 0,
        1,
        jnp.where(distance == 2, 3, jnp.where((distance == 3) | at_end, 0, 2)),
    )
    rank = rank_in_slot(slot)
    k = place_of ^ place
    back = jnp.where(
        kind < 3,
        (k * 3 + kind) * capacity + rank,
        (3 * PLANE + here + place_of) * capacity + rank,
    )
    passed = (3 * PLANE + PLANE - here + place_of) * capacity + rank
    back = jnp.where((kind == 0) & ~inner, passed, back)

    weights = join(down, up)
    outward, middle = send(weights, to_outward), send(weights, to_middle)
    first = pack_first(
        jnp.where(kind == 0, (k - 1) * capacity + rank, -1), hidden, capacity, PLANE - 1
    )
    to_rest = jnp.where(kind == 0, jnp.where(k == 0, 0, -1), 1 + (kind - 1) * PLANE + k)
    to_rest = jnp.where(to_rest < 0, -1, to_rest * capacity + rank)
    kept, *rest = pack(to_rest, hidden, [capacity] * (1 + 3 * PLANE), LONG)
    own, near, far = (rest[i * PLANE : (i + 1) * PLANE] for i in range(3))
    first, own = lax.optimization_barrier((exchange([kept, *first]), own))
    own = exchange(own)
    done = meanwhile()
    outward, middle, done = lax.optimization_barrier((outward, middle, done))
    middle = choose(where, middle, first)
    own, near, outward, middle = lax.optimization_barrier((own, near, outward, middle))
    middle2, swapped = send(outward, to_middle), send(middle, to_outward)
    near, far = lax.optimization_barrier((exchange(near), far))
    far = exchange(far)
    rows = [*first, *own, *near]
    soon = early(where, rows, outward, middle, weights, capacity)
    soon, where = lax.optimization_barrier((soon, where))
    soon = exchange(soon)
    last = gather(late(where, far, middle2, swapped, capacity), 2 * PLANE)
    return back, [*soon, last], done


def by_rows(hidden, slot, down, up, capacity, meanwhile):
    devices = lax.axis_size("adapter")
    target = slot * capacity + rank_in_slot(slot)
    spots = jnp.arange(devices * capacity, dtype=jnp.int32)
    placing = (target[None, :] == spots[:, None]).astype(jnp.bfloat16)
    outgoing = jnp.dot(placing, hidden, preferred_element_type=jnp.float32).astype(jnp.bfloat16)
    outgoing = outgoing.reshape(devices, capacity, hidden.shape[1])
    incoming = lax.all_to_all(outgoing, "adapter", split_axis=0, concat_axis=0, tiled=True)
    rows = incoming.reshape(-1, hidden.shape[1])
    shrunk = lax.dot_general(rows, down, NT, preferred_element_type=jnp.float32)
    wide = expand(shrunk, up)
    returned = lax.all_to_all(
        wide.reshape(devices, capacity, -1), "adapter", split_axis=0, concat_axis=0, tiled=True
    )
    return target, [returned.reshape(devices * capacity, -1)], meanwhile()


def on_device(
    hidden,
    queries,
    base_key_value,
    key_value_cache,
    lengths,
    request_adapter_index,
    adapter_position_map,
    adapter_down_weight,
    adapter_up_weight,
):
    devices = lax.axis_size("adapter")
    capacity = max(2, 2 * hidden.shape[0] // devices)
    slot = slot_lookup(request_adapter_index[:, 0], adapter_position_map)
    deliver = by_planes if devices == 4 * PLANE else by_rows
    meanwhile = lambda: cached_attention(queries, key_value_cache, lengths)
    target, pieces, (mixed, logs) = deliver(
        hidden, slot, adapter_down_weight[0], adapter_up_weight[0], capacity, meanwhile
    )
    return finish(target, base_key_value, queries, mixed, logs, pieces)


def solution(mesh):
    rows = P(("groups", "adapter"), None)
    deep = P(("groups", "adapter"), None, None)
    placed = (
        rows,
        rows,
        rows,
        deep,
        P(("groups", "adapter")),
        rows,
        P("groups"),
        deep,
        deep,
    )
    return jax.shard_map(
        on_device, mesh=mesh, in_specs=placed, out_specs=(rows, rows), check_vma=False
    )
```

```python
import functools

import jax
import jax.numpy as jnp
from jax import lax
from jax.experimental import pallas as pl
from jax.experimental.pallas import tpu as pltpu
from jax.sharding import PartitionSpec as P

QUERY_HEADS = 32
KEY_VALUE_HEADS = 4
HEAD_SIZE = 128
GROUP = QUERY_HEADS // KEY_VALUE_HEADS
SPLIT = KEY_VALUE_HEADS * HEAD_SIZE
PLANE = 4
COLS = 2048
LONG = 20_000_000_000

adapter_scale = 2.0
score_floor = -1e30
score_scale = HEAD_SIZE ** (-0.5)

NT = (((1,), (1,)), ((), ()))


def slot_lookup(request_adapter, adapter_position_map):
    adapter_index = jnp.arange(adapter_position_map.shape[0], dtype=jnp.int32)
    matches = request_adapter[:, None] == adapter_index[None, :]
    return jnp.sum(jnp.where(matches, adapter_position_map[None, :], 0), axis=1)


def rank_in_slot(slot):
    order = jnp.arange(slot.shape[0], dtype=jnp.int32)
    same = slot[:, None] == slot[None, :]
    before = order[None, :] < order[:, None]
    return jnp.sum((same & before).astype(jnp.int32), axis=1)


VMEM = pl.BlockSpec(memory_space=pltpu.VMEM)
SMEM = pl.BlockSpec(memory_space=pltpu.SMEM)
HBM = pl.BlockSpec(memory_space=pltpu.HBM)


def options(name, cost=None, mebibytes=12):
    chosen = dict(
        name=name,
        compiler_params=pltpu.CompilerParams(vmem_limit_bytes=mebibytes * 1024 * 1024),
    )
    if cost is not None:
        chosen["cost_estimate"] = pl.CostEstimate(
            flops=1000, bytes_accessed=cost, transcendentals=0
        )
    return chosen


def chunks(width):
    return [slice(c, c + COLS) for c in range(0, width, COLS)]


def cached_kernel(step, length_ref, q_ref, cache_ref, mixed_ref, log_ref):
    total, context = cache_ref.shape[0], cache_ref.shape[1]
    keys = step * context
    owner_q = lax.rem(lax.broadcasted_iota(jnp.int32, (GROUP * step, keys), 0), step)
    column = lax.broadcasted_iota(jnp.int32, (GROUP * step, keys), 1)
    owner_k, position = column // context, lax.rem(column, context)
    lane = lax.broadcasted_iota(jnp.int32, (step, HEAD_SIZE), 1)

    def requests(i, carry):
        rows = pl.ds(pl.multiple_of(i * step, step), step)
        lengths = jnp.concatenate([length_ref[rows, :]] * GROUP, axis=0)
        included = (owner_q == owner_k) & (position < lengths)
        logs = jnp.zeros((step, HEAD_SIZE), jnp.float32)
        for head in range(KEY_VALUE_HEADS):
            first = head * GROUP
            q = jnp.concatenate(
                [
                    q_ref[rows, (first + g) * HEAD_SIZE : (first + g + 1) * HEAD_SIZE]
                    for g in range(GROUP)
                ],
                axis=0,
            )
            k = cache_ref[rows, :, head * HEAD_SIZE : (head + 1) * HEAD_SIZE]
            v = cache_ref[rows, :, SPLIT + head * HEAD_SIZE : SPLIT + (head + 1) * HEAD_SIZE]
            k, v = k.reshape(keys, HEAD_SIZE), v.reshape(keys, HEAD_SIZE)
            score = lax.dot_general(q, k, NT, preferred_element_type=jnp.float32) * score_scale
            score = jnp.where(included, score, score_floor)
            peak = jnp.max(score, axis=1, keepdims=True)
            weight = jnp.exp(score - peak)
            denominator = jnp.sum(weight, axis=1, keepdims=True)
            mixed = jnp.dot(weight.astype(jnp.bfloat16), v, preferred_element_type=jnp.float32)
            mixed = (mixed / denominator).astype(jnp.bfloat16)
            log = peak + jnp.log(denominator)
            for g in range(GROUP):
                part = slice(g * step, (g + 1) * step)
                mixed_ref[rows, (first + g) * HEAD_SIZE : (first + g + 1) * HEAD_SIZE] = mixed[
                    part
                ]
                logs = jnp.where(lane == first + g, log[part], logs)
        log_ref[rows, :] = logs
        return carry

    lax.fori_loop(0, total // step, requests, 0)


def cached_attention(queries, cache, lengths):
    rows = cache.shape[0]
    return pl.pallas_call(
        functools.partial(cached_kernel, 16),
        in_specs=[VMEM] * 3,
        out_specs=[VMEM] * 2,
        out_shape=[
            jax.ShapeDtypeStruct(queries.shape, jnp.bfloat16),
            jax.ShapeDtypeStruct((rows, HEAD_SIZE), jnp.float32),
        ],
        **options("cached", LONG),
    )(lengths.reshape(rows, 1), queries, cache)


def finish_kernel(count, target_ref, log_ref, base_hbm, q_hbm, mixed_hbm, *refs):
    pieces, refs = refs[:count], refs[count:]
    attention_hbm, written_hbm, attention_ref, written_ref, stack_ref, mixed_ref = refs[:6]
    base_ref, q_ref, sems, piece_sems, mixed_sems = refs[6:]
    rows = base_ref.shape[0]
    base_copy = pltpu.make_async_copy(base_hbm, base_ref, piece_sems.at[count])
    base_copy.start()
    total = stack_ref.shape[0]
    arrivals, start = [], 0
    for i, piece in enumerate(pieces):
        spot = stack_ref.at[start : start + piece.shape[0]]
        arrivals.append(pltpu.make_async_copy(piece, spot, piece_sems.at[i]))
        arrivals[-1].start()
        start += piece.shape[0]
    spots = lax.broadcasted_iota(jnp.int32, (rows, total), 1)
    place = (spots == target_ref[...]).astype(jnp.float32).astype(jnp.bfloat16)
    mixes = []
    for head in range(KEY_VALUE_HEADS):
        wide = slice(head * GROUP * HEAD_SIZE, (head + 1) * GROUP * HEAD_SIZE)
        pair = (
            pltpu.make_async_copy(q_hbm.at[:, wide], q_ref.at[:, wide], mixed_sems.at[0, head]),
            pltpu.make_async_copy(
                mixed_hbm.at[:, wide], mixed_ref.at[:, wide], mixed_sems.at[1, head]
            ),
        )
        for copy in pair:
            copy.start()
        mixes.append(pair)
    for arrival in arrivals:
        arrival.wait()
    base_copy.wait()
    delta = jnp.dot(place, stack_ref[...], preferred_element_type=jnp.float32)
    written_ref[...] = (base_ref[...].astype(jnp.float32) + delta).astype(jnp.bfloat16)
    copies = [pltpu.make_async_copy(written_ref, written_hbm, sems.at[KEY_VALUE_HEADS])]
    copies[0].start()
    lane = lax.broadcasted_iota(jnp.int32, (rows, HEAD_SIZE), 1)
    logs = log_ref[...]
    for head in range(KEY_VALUE_HEADS):
        own = slice(head * HEAD_SIZE, (head + 1) * HEAD_SIZE)
        new_key = written_ref[:, own].astype(jnp.float32)
        own = slice(SPLIT + head * HEAD_SIZE, SPLIT + (head + 1) * HEAD_SIZE)
        new_value = written_ref[:, own].astype(jnp.float32)
        for copy in mixes[head]:
            copy.wait()
        for i in range(head * GROUP, (head + 1) * GROUP):
            part = slice(i * HEAD_SIZE, (i + 1) * HEAD_SIZE)
            query = q_ref[:, part].astype(jnp.float32)
            score = jnp.sum(query * new_key, axis=1, keepdims=True) * score_scale
            log = jnp.sum(jnp.where(lane == i, logs, 0.0), axis=1, keepdims=True)
            share = 1.0 / (1.0 + jnp.exp(score - log))
            out = new_value + share * (mixed_ref[:, part].astype(jnp.float32) - new_value)
            attention_ref[:, part] = out.astype(jnp.bfloat16)
        wide = slice(head * GROUP * HEAD_SIZE, (head + 1) * GROUP * HEAD_SIZE)
        copies.append(
            pltpu.make_async_copy(
                attention_ref.at[:, wide], attention_hbm.at[:, wide], sems.at[head]
            )
        )
        copies[-1].start()
    for copy in copies:
        copy.wait()


def finish(target, base, queries, mixed, logs, pieces):
    rows = base.shape[0]
    return pl.pallas_call(
        functools.partial(finish_kernel, len(pieces)),
        in_specs=[VMEM] * 2 + [HBM] * (3 + len(pieces)),
        out_specs=[HBM] * 2,
        out_shape=[
            jax.ShapeDtypeStruct(queries.shape, jnp.bfloat16),
            jax.ShapeDtypeStruct(base.shape, jnp.bfloat16),
        ],
        scratch_shapes=[
            pltpu.VMEM(queries.shape, jnp.bfloat16),
            pltpu.VMEM(base.shape, jnp.bfloat16),
            pltpu.VMEM((sum(piece.shape[0] for piece in pieces), base.shape[1]), jnp.bfloat16),
            pltpu.VMEM(mixed.shape, mixed.dtype),
            pltpu.VMEM(base.shape, base.dtype),
            pltpu.VMEM(queries.shape, queries.dtype),
            pltpu.SemaphoreType.DMA((KEY_VALUE_HEADS + 1,)),
            pltpu.SemaphoreType.DMA((len(pieces) + 1,)),
            pltpu.SemaphoreType.DMA((2, KEY_VALUE_HEADS)),
        ],
        **options("finish", 1000, 60),
    )(target.reshape(rows, 1), logs, base, queries, mixed, *pieces)


def pack_kernel(target_ref, hidden_hbm, *refs):
    outs, (hidden_ref, packed_ref, hidden_sems, sems) = refs[:-4], refs[-4:]
    spots = packed_ref.shape[0]
    parts = chunks(hidden_ref.shape[1])
    fetches, stores = [], []
    for i, part in enumerate(parts):
        fetches.append(
            pltpu.make_async_copy(
                hidden_hbm.at[:, part], hidden_ref.at[:, part], hidden_sems.at[i]
            )
        )
        fetches[-1].start()
    spot = lax.broadcasted_iota(jnp.int32, (spots, hidden_ref.shape[0]), 0)
    place = (spot == target_ref[...]).astype(jnp.float32).astype(jnp.bfloat16)
    for i, part in enumerate(parts):
        fetches[i].wait()
        packed = jnp.dot(place, hidden_ref[:, part], preferred_element_type=jnp.float32)
        packed_ref[:, part] = packed.astype(jnp.bfloat16)
        start = 0
        for j, out in enumerate(outs):
            own = packed_ref.at[start : start + out.shape[0], part]
            stores.append(pltpu.make_async_copy(own, out.at[:, part], sems.at[i, j]))
            stores[-1].start()
            start += out.shape[0]
    for store in stores:
        store.wait()


def pack(target, hidden, heights, cost):
    rows, width = hidden.shape
    steps = len(chunks(width))
    return pl.pallas_call(
        pack_kernel,
        in_specs=[VMEM, HBM],
        out_specs=[HBM] * len(heights),
        out_shape=[jax.ShapeDtypeStruct((height, width), jnp.bfloat16) for height in heights],
        scratch_shapes=[
            pltpu.VMEM(hidden.shape, jnp.bfloat16),
            pltpu.VMEM((sum(heights), width), jnp.bfloat16),
            pltpu.SemaphoreType.DMA((steps,)),
            pltpu.SemaphoreType.DMA((steps, len(heights))),
        ],
        **options("pack", cost, 60),
    )(target.reshape(1, rows), hidden)


def pack_first_kernel(target_ref, hidden_ref, *outs):
    height = outs[0].shape[0]
    spot = lax.broadcasted_iota(jnp.int32, (height * len(outs), hidden_ref.shape[0]), 0)
    place = (spot == target_ref[...]).astype(jnp.float32).astype(jnp.bfloat16)
    for part in chunks(hidden_ref.shape[1]):
        packed = jnp.dot(place, hidden_ref[:, part], preferred_element_type=jnp.float32)
        packed = packed.astype(jnp.bfloat16)
        for i, out in enumerate(outs):
            out[:, part] = packed[i * height : (i + 1) * height]


def pack_first(target, hidden, height, count):
    rows, width = hidden.shape
    return pl.pallas_call(
        pack_first_kernel,
        in_specs=[VMEM] * 2,
        out_specs=[VMEM] * count,
        out_shape=[jax.ShapeDtypeStruct((height, width), jnp.bfloat16)] * count,
        **options("first"),
    )(target.reshape(1, rows), hidden)


def expand(total, up):
    shrunk = total.astype(jnp.bfloat16)
    wide = jnp.dot(shrunk, up, preferred_element_type=jnp.float32)
    return (adapter_scale * wide).astype(jnp.bfloat16)


def shrink(row_parts, downs):
    total = None
    for part in chunks(row_parts[0].shape[1]):
        rows = jnp.concatenate([ref[:, part] for ref in row_parts], axis=0)
        down = jnp.concatenate([ref[:, part] for ref in downs], axis=0)
        product = lax.dot_general(rows, down, NT, preferred_element_type=jnp.float32)
        total = product if total is None else total + product
    return total


def put(out, dest, slots, slot, rows):
    height = rows.shape[0]
    start = pl.multiple_of((dest * slots + slot) * height, height)
    out[pl.ds(start, height), :] = rows


def join_kernel(down_hbm, up_hbm, out_ref, sems):
    width = down_hbm.shape[1]
    down = pltpu.make_async_copy(down_hbm, out_ref.at[:, :width], sems.at[0])
    up = pltpu.make_async_copy(up_hbm, out_ref.at[:, width:], sems.at[1])
    down.start()
    up.start()
    down.wait()
    up.wait()


def join(down, up):
    return pl.pallas_call(
        join_kernel,
        in_specs=[HBM] * 2,
        out_specs=VMEM,
        out_shape=jax.ShapeDtypeStruct((down.shape[0], down.shape[1] + up.shape[1]), down.dtype),
        scratch_shapes=[pltpu.SemaphoreType.DMA((2,))],
        **options("join", 1000, 60),
    )(down, up)


def early_kernel(capacity, where_ref, *refs):
    rows, (outward, middle, own, *outs) = refs[: 3 * PLANE], refs[3 * PLANE :]
    width, rank = rows[0].shape[1], own.shape[0]

    def run(weights):
        total = shrink(rows, weights)
        for slot, weight in enumerate(weights):
            start = slot * PLANE * capacity
            sums = total[start : start + PLANE * capacity, slot * rank : (slot + 1) * rank]
            wide = expand(sums, weight[:, width:])
            for k, out in enumerate(outs):
                out[slot * capacity : (slot + 1) * capacity] = wide[
                    k * capacity : (k + 1) * capacity
                ]

    pl.when(where_ref[0] == 1)(lambda: run([outward, own, middle]))
    pl.when(where_ref[0] == 0)(lambda: run([outward, own, outward]))


def early(where, rows, outward, middle, own, capacity):
    out_width = own.shape[1] - rows[0].shape[1]
    return pl.pallas_call(
        functools.partial(early_kernel, capacity),
        in_specs=[SMEM] + [VMEM] * (3 * PLANE + 3),
        out_specs=[VMEM] * PLANE,
        out_shape=[jax.ShapeDtypeStruct((3 * capacity, out_width), jnp.bfloat16)] * PLANE,
        **options("early", 1000),
    )(where, *rows, outward, middle, own)


def late_kernel(capacity, where_ref, *refs):
    rows, (middle2, swapped, out) = refs[:PLANE], refs[PLANE:]
    width = rows[0].shape[1]
    place, here, there = where_ref[1], where_ref[2], where_ref[3]

    def spread(first, wide):
        for k in range(PLANE):
            put(out, first + (place ^ k), 1, 0, wide[k * capacity : (k + 1) * capacity])

    @pl.when(where_ref[0] == 1)
    def _():
        total = shrink([*rows, swapped], [middle2])
        wide = expand(total, middle2[:, width:])
        spread(here, wide)
        spread(there, wide[PLANE * capacity :])

    @pl.when(where_ref[0] == 0)
    def _():
        wide = expand(shrink(rows, [swapped]), swapped[:, width:])
        spread(here, wide)
        spread(there, jnp.zeros(wide.shape, wide.dtype))


def late(where, rows, middle2, swapped, capacity):
    out_width = swapped.shape[1] - rows[0].shape[1]
    return pl.pallas_call(
        functools.partial(late_kernel, capacity),
        in_specs=[SMEM] + [VMEM] * (PLANE + 2),
        out_specs=VMEM,
        out_shape=jax.ShapeDtypeStruct((2 * PLANE * capacity, out_width), jnp.bfloat16),
        **options("late"),
    )(where, *rows, middle2, swapped)


def choose_kernel(where_ref, weights_hbm, *refs):
    rows, (out_hbm, stack_ref, sems) = refs[:PLANE], refs[PLANE:]
    capacity, width = stack_ref.shape[0] // PLANE, stack_ref.shape[1]

    @pl.when(where_ref[0] == 0)
    def _():
        copies = []
        for k, ref in enumerate(rows):
            for i, part in enumerate(chunks(width)):
                here = stack_ref.at[k * capacity : (k + 1) * capacity, part]
                there = out_hbm.at[k * capacity : (k + 1) * capacity, part]
                fetch = pltpu.make_async_copy(ref.at[:, part], here, sems.at[0, k, i])
                copies.append((fetch, pltpu.make_async_copy(here, there, sems.at[1, k, i])))
                fetch.start()
        for fetch, store in copies:
            fetch.wait()
            store.start()
        for _, store in copies:
            store.wait()


def choose(where, weights, rows):
    height, width = rows[0].shape
    return pl.pallas_call(
        choose_kernel,
        in_specs=[SMEM] + [HBM] * (1 + PLANE),
        out_specs=HBM,
        out_shape=jax.ShapeDtypeStruct(weights.shape, weights.dtype),
        scratch_shapes=[
            pltpu.VMEM((height * PLANE, width), weights.dtype),
            pltpu.SemaphoreType.DMA((2, PLANE, len(chunks(width)))),
        ],
        input_output_aliases={1: 0},
        **options("choose", 1000, 60),
    )(where, weights, *rows)


def by_planes(hidden, slot, down, up, capacity, meanwhile):
    devices = lax.axis_size("adapter")
    me = lax.axis_index("adapter")
    plane, place = me // PLANE, me % PLANE
    inner = (plane == 1) | (plane == 2)
    here = plane % 2 * PLANE
    where = jnp.stack([inner.astype(jnp.int32), place, here, PLANE - here]).astype(jnp.int32)
    all_devices = range(devices)
    middles = [i for i in all_devices if i // PLANE in (1, 2)]
    across = [
        [(i, (i // PLANE) * PLANE + ((i % PLANE) ^ k)) for i in all_devices] for k in range(PLANE)
    ]
    to_outward = [(i, i ^ PLANE) for i in all_devices]
    to_middle = [(i, i ^ (3 * PLANE)) for i in middles]
    send = lambda a, pairs: lax.ppermute(a, "adapter", pairs)

    def gather(rows, size):
        parts = rows.reshape(size, -1, rows.shape[1])
        groups = [list(range(i, i + size)) for i in range(0, devices, size)]
        parts = lax.all_to_all(parts, "adapter", 0, 0, axis_index_groups=groups, tiled=True)
        return parts.reshape(rows.shape)

    exchange = lambda parts: [parts[0]] + [send(parts[k], across[k]) for k in range(1, PLANE)]

    plane_of, place_of = slot // PLANE, slot % PLANE
    distance = jnp.abs(plane_of - plane)
    at_end = (plane_of == 0) | (plane_of == 3)
    kind = jnp.where(
        distance == 0,
        1,
        jnp.where(distance == 2, 3, jnp.where((distance == 3) | at_end, 0, 2)),
    )
    rank = rank_in_slot(slot)
    k = place_of ^ place
    back = jnp.where(
        kind < 3,
        (k * 3 + kind) * capacity + rank,
        (3 * PLANE + here + place_of) * capacity + rank,
    )
    passed = (3 * PLANE + PLANE - here + place_of) * capacity + rank
    back = jnp.where((kind == 0) & ~inner, passed, back)

    weights = join(down, up)
    outward, middle = send(weights, to_outward), send(weights, to_middle)
    first = pack_first(
        jnp.where(kind == 0, (k - 1) * capacity + rank, -1), hidden, capacity, PLANE - 1
    )
    to_rest = jnp.where(kind == 0, jnp.where(k == 0, 0, -1), 1 + (kind - 1) * PLANE + k)
    to_rest = jnp.where(to_rest < 0, -1, to_rest * capacity + rank)
    kept, *rest = pack(to_rest, hidden, [capacity] * (1 + 3 * PLANE), LONG)
    own, near, far = (rest[i * PLANE : (i + 1) * PLANE] for i in range(3))
    first, own = lax.optimization_barrier((exchange([kept, *first]), own))
    own = exchange(own)
    done = meanwhile()
    middle = choose(where, middle, first)
    own, near, middle = lax.optimization_barrier((own, near, middle))
    middle2, swapped = send(outward, to_middle), send(middle, to_outward)
    near, far, done = lax.optimization_barrier((exchange(near), far, done))
    far = exchange(far)
    rows = [*first, *own, *near]
    soon = early(where, rows, outward, middle, weights, capacity)
    soon, where = lax.optimization_barrier((soon, where))
    soon = exchange(soon)
    last = late(where, far, middle2, swapped, capacity)
    soon, last = lax.optimization_barrier((soon, last))
    last = gather(last, 2 * PLANE)
    return back, [*soon, last], done


def by_rows(hidden, slot, down, up, capacity, meanwhile):
    devices = lax.axis_size("adapter")
    target = slot * capacity + rank_in_slot(slot)
    spots = jnp.arange(devices * capacity, dtype=jnp.int32)
    placing = (target[None, :] == spots[:, None]).astype(jnp.bfloat16)
    outgoing = jnp.dot(placing, hidden, preferred_element_type=jnp.float32).astype(jnp.bfloat16)
    outgoing = outgoing.reshape(devices, capacity, hidden.shape[1])
    incoming = lax.all_to_all(outgoing, "adapter", split_axis=0, concat_axis=0, tiled=True)
    rows = incoming.reshape(-1, hidden.shape[1])
    shrunk = lax.dot_general(rows, down, NT, preferred_element_type=jnp.float32)
    wide = expand(shrunk, up)
    returned = lax.all_to_all(
        wide.reshape(devices, capacity, -1), "adapter", split_axis=0, concat_axis=0, tiled=True
    )
    return target, [returned.reshape(devices * capacity, -1)], meanwhile()


def on_device(
    hidden,
    queries,
    base_key_value,
    key_value_cache,
    lengths,
    request_adapter_index,
    adapter_position_map,
    adapter_down_weight,
    adapter_up_weight,
):
    devices = lax.axis_size("adapter")
    capacity = max(2, 2 * hidden.shape[0] // devices)
    slot = slot_lookup(request_adapter_index[:, 0], adapter_position_map)
    deliver = by_planes if devices == 4 * PLANE else by_rows
    meanwhile = lambda: cached_attention(queries, key_value_cache, lengths)
    target, pieces, (mixed, logs) = deliver(
        hidden, slot, adapter_down_weight[0], adapter_up_weight[0], capacity, meanwhile
    )
    return finish(target, base_key_value, queries, mixed, logs, pieces)


def solution(mesh):
    rows = P(("groups", "adapter"), None)
    deep = P(("groups", "adapter"), None, None)
    placed = (
        rows,
        rows,
        rows,
        deep,
        P(("groups", "adapter")),
        rows,
        P("groups"),
        deep,
        deep,
    )
    return jax.shard_map(
        on_device, mesh=mesh, in_specs=placed, out_specs=(rows, rows), check_vma=False
    )
```

```python
import functools

import jax
import jax.numpy as jnp
from jax import lax
from jax.experimental import pallas as pl
from jax.experimental.pallas import tpu as pltpu
from jax.sharding import PartitionSpec as P

QUERY_HEADS = 32
KEY_VALUE_HEADS = 4
HEAD_SIZE = 128
GROUP = QUERY_HEADS // KEY_VALUE_HEADS
SPLIT = KEY_VALUE_HEADS * HEAD_SIZE
PLANE = 4
COLS = 2048
LONG = 20_000_000_000

adapter_scale = 2.0
score_floor = -1e30
score_scale = HEAD_SIZE ** (-0.5)

NT = (((1,), (1,)), ((), ()))


def slot_lookup(request_adapter, adapter_position_map):
    adapter_index = jnp.arange(adapter_position_map.shape[0], dtype=jnp.int32)
    matches = request_adapter[:, None] == adapter_index[None, :]
    return jnp.sum(jnp.where(matches, adapter_position_map[None, :], 0), axis=1)


def rank_in_slot(slot):
    order = jnp.arange(slot.shape[0], dtype=jnp.int32)
    same = slot[:, None] == slot[None, :]
    before = order[None, :] < order[:, None]
    return jnp.sum((same & before).astype(jnp.int32), axis=1)


VMEM = pl.BlockSpec(memory_space=pltpu.VMEM)
SMEM = pl.BlockSpec(memory_space=pltpu.SMEM)
HBM = pl.BlockSpec(memory_space=pltpu.HBM)


def options(name, cost=None, mebibytes=12):
    chosen = dict(
        name=name,
        compiler_params=pltpu.CompilerParams(vmem_limit_bytes=mebibytes * 1024 * 1024),
    )
    if cost is not None:
        chosen["cost_estimate"] = pl.CostEstimate(
            flops=1000, bytes_accessed=cost, transcendentals=0
        )
    return chosen


def chunks(width):
    return [slice(c, c + COLS) for c in range(0, width, COLS)]


def cached_kernel(step, length_ref, q_ref, cache_ref, mixed_ref, log_ref):
    total, context = cache_ref.shape[0], cache_ref.shape[1]
    keys = step * context
    owner_q = lax.rem(lax.broadcasted_iota(jnp.int32, (GROUP * step, keys), 0), step)
    column = lax.broadcasted_iota(jnp.int32, (GROUP * step, keys), 1)
    owner_k, position = column // context, lax.rem(column, context)
    lane = lax.broadcasted_iota(jnp.int32, (step, HEAD_SIZE), 1)

    def requests(i, carry):
        rows = pl.ds(pl.multiple_of(i * step, step), step)
        lengths = jnp.concatenate([length_ref[rows, :]] * GROUP, axis=0)
        included = (owner_q == owner_k) & (position < lengths)
        logs = jnp.zeros((step, HEAD_SIZE), jnp.float32)
        for head in range(KEY_VALUE_HEADS):
            first = head * GROUP
            q = jnp.concatenate(
                [
                    q_ref[rows, (first + g) * HEAD_SIZE : (first + g + 1) * HEAD_SIZE]
                    for g in range(GROUP)
                ],
                axis=0,
            )
            k = cache_ref[rows, :, head * HEAD_SIZE : (head + 1) * HEAD_SIZE]
            v = cache_ref[rows, :, SPLIT + head * HEAD_SIZE : SPLIT + (head + 1) * HEAD_SIZE]
            k, v = k.reshape(keys, HEAD_SIZE), v.reshape(keys, HEAD_SIZE)
            score = lax.dot_general(q, k, NT, preferred_element_type=jnp.float32) * score_scale
            score = jnp.where(included, score, score_floor)
            peak = jnp.max(score, axis=1, keepdims=True)
            weight = jnp.exp(score - peak)
            denominator = jnp.sum(weight, axis=1, keepdims=True)
            mixed = jnp.dot(weight.astype(jnp.bfloat16), v, preferred_element_type=jnp.float32)
            mixed = (mixed / denominator).astype(jnp.bfloat16)
            log = peak + jnp.log(denominator)
            for g in range(GROUP):
                part = slice(g * step, (g + 1) * step)
                mixed_ref[rows, (first + g) * HEAD_SIZE : (first + g + 1) * HEAD_SIZE] = mixed[
                    part
                ]
                logs = jnp.where(lane == first + g, log[part], logs)
        log_ref[rows, :] = logs
        return carry

    lax.fori_loop(0, total // step, requests, 0)


def cached_attention(queries, cache, lengths):
    rows = cache.shape[0]
    return pl.pallas_call(
        functools.partial(cached_kernel, 16),
        in_specs=[VMEM] * 3,
        out_specs=[VMEM] * 2,
        out_shape=[
            jax.ShapeDtypeStruct(queries.shape, jnp.bfloat16),
            jax.ShapeDtypeStruct((rows, HEAD_SIZE), jnp.float32),
        ],
        **options("cached", LONG),
    )(lengths.reshape(rows, 1), queries, cache)


def finish_kernel(count, target_ref, log_ref, base_hbm, q_hbm, mixed_hbm, *refs):
    pieces, refs = refs[:count], refs[count:]
    attention_hbm, written_hbm, attention_ref, written_ref, stack_ref, mixed_ref = refs[:6]
    base_ref, q_ref, sems, piece_sems, mixed_sems = refs[6:]
    rows = base_ref.shape[0]
    base_copy = pltpu.make_async_copy(base_hbm, base_ref, piece_sems.at[count])
    base_copy.start()
    total = stack_ref.shape[0]
    arrivals, start = [], 0
    for i, piece in enumerate(pieces):
        spot = stack_ref.at[start : start + piece.shape[0]]
        arrivals.append(pltpu.make_async_copy(piece, spot, piece_sems.at[i]))
        arrivals[-1].start()
        start += piece.shape[0]
    spots = lax.broadcasted_iota(jnp.int32, (rows, total), 1)
    place = (spots == target_ref[...]).astype(jnp.float32).astype(jnp.bfloat16)
    mixes = []
    for head in range(KEY_VALUE_HEADS):
        wide = slice(head * GROUP * HEAD_SIZE, (head + 1) * GROUP * HEAD_SIZE)
        pair = (
            pltpu.make_async_copy(q_hbm.at[:, wide], q_ref.at[:, wide], mixed_sems.at[0, head]),
            pltpu.make_async_copy(
                mixed_hbm.at[:, wide], mixed_ref.at[:, wide], mixed_sems.at[1, head]
            ),
        )
        for copy in pair:
            copy.start()
        mixes.append(pair)
    for arrival in arrivals:
        arrival.wait()
    base_copy.wait()
    delta = jnp.dot(place, stack_ref[...], preferred_element_type=jnp.float32)
    written_ref[...] = (base_ref[...].astype(jnp.float32) + delta).astype(jnp.bfloat16)
    copies = [pltpu.make_async_copy(written_ref, written_hbm, sems.at[KEY_VALUE_HEADS])]
    copies[0].start()
    lane = lax.broadcasted_iota(jnp.int32, (rows, HEAD_SIZE), 1)
    logs = log_ref[...]
    for head in range(KEY_VALUE_HEADS):
        own = slice(head * HEAD_SIZE, (head + 1) * HEAD_SIZE)
        new_key = written_ref[:, own].astype(jnp.float32)
        own = slice(SPLIT + head * HEAD_SIZE, SPLIT + (head + 1) * HEAD_SIZE)
        new_value = written_ref[:, own].astype(jnp.float32)
        for copy in mixes[head]:
            copy.wait()
        for i in range(head * GROUP, (head + 1) * GROUP):
            part = slice(i * HEAD_SIZE, (i + 1) * HEAD_SIZE)
            query = q_ref[:, part].astype(jnp.float32)
            score = jnp.sum(query * new_key, axis=1, keepdims=True) * score_scale
            log = jnp.sum(jnp.where(lane == i, logs, 0.0), axis=1, keepdims=True)
            share = 1.0 / (1.0 + jnp.exp(score - log))
            out = new_value + share * (mixed_ref[:, part].astype(jnp.float32) - new_value)
            attention_ref[:, part] = out.astype(jnp.bfloat16)
        wide = slice(head * GROUP * HEAD_SIZE, (head + 1) * GROUP * HEAD_SIZE)
        copies.append(
            pltpu.make_async_copy(
                attention_ref.at[:, wide], attention_hbm.at[:, wide], sems.at[head]
            )
        )
        copies[-1].start()
    for copy in copies:
        copy.wait()


def finish(target, base, queries, mixed, logs, pieces):
    rows = base.shape[0]
    return pl.pallas_call(
        functools.partial(finish_kernel, len(pieces)),
        in_specs=[VMEM] * 2 + [HBM] * (3 + len(pieces)),
        out_specs=[HBM] * 2,
        out_shape=[
            jax.ShapeDtypeStruct(queries.shape, jnp.bfloat16),
            jax.ShapeDtypeStruct(base.shape, jnp.bfloat16),
        ],
        scratch_shapes=[
            pltpu.VMEM(queries.shape, jnp.bfloat16),
            pltpu.VMEM(base.shape, jnp.bfloat16),
            pltpu.VMEM((sum(piece.shape[0] for piece in pieces), base.shape[1]), jnp.bfloat16),
            pltpu.VMEM(mixed.shape, mixed.dtype),
            pltpu.VMEM(base.shape, base.dtype),
            pltpu.VMEM(queries.shape, queries.dtype),
            pltpu.SemaphoreType.DMA((KEY_VALUE_HEADS + 1,)),
            pltpu.SemaphoreType.DMA((len(pieces) + 1,)),
            pltpu.SemaphoreType.DMA((2, KEY_VALUE_HEADS)),
        ],
        **options("finish", 1000, 60),
    )(target.reshape(rows, 1), logs, base, queries, mixed, *pieces)


def pack_kernel(target_ref, hidden_hbm, *refs):
    outs, (hidden_ref, packed_ref, hidden_sems, sems) = refs[:-4], refs[-4:]
    spots = packed_ref.shape[0]
    parts = chunks(hidden_ref.shape[1])
    fetches, stores = [], []
    for i, part in enumerate(parts):
        fetches.append(
            pltpu.make_async_copy(
                hidden_hbm.at[:, part], hidden_ref.at[:, part], hidden_sems.at[i]
            )
        )
        fetches[-1].start()
    spot = lax.broadcasted_iota(jnp.int32, (spots, hidden_ref.shape[0]), 0)
    place = (spot == target_ref[...]).astype(jnp.float32).astype(jnp.bfloat16)
    for i, part in enumerate(parts):
        fetches[i].wait()
        packed = jnp.dot(place, hidden_ref[:, part], preferred_element_type=jnp.float32)
        packed_ref[:, part] = packed.astype(jnp.bfloat16)
        start = 0
        for j, out in enumerate(outs):
            own = packed_ref.at[start : start + out.shape[0], part]
            stores.append(pltpu.make_async_copy(own, out.at[:, part], sems.at[i, j]))
            stores[-1].start()
            start += out.shape[0]
    for store in stores:
        store.wait()


def pack(target, hidden, heights, cost):
    rows, width = hidden.shape
    steps = len(chunks(width))
    return pl.pallas_call(
        pack_kernel,
        in_specs=[VMEM, HBM],
        out_specs=[HBM] * len(heights),
        out_shape=[jax.ShapeDtypeStruct((height, width), jnp.bfloat16) for height in heights],
        scratch_shapes=[
            pltpu.VMEM(hidden.shape, jnp.bfloat16),
            pltpu.VMEM((sum(heights), width), jnp.bfloat16),
            pltpu.SemaphoreType.DMA((steps,)),
            pltpu.SemaphoreType.DMA((steps, len(heights))),
        ],
        **options("pack", cost, 60),
    )(target.reshape(1, rows), hidden)


def pack_first_kernel(target_ref, hidden_ref, *outs):
    height = outs[0].shape[0]
    spot = lax.broadcasted_iota(jnp.int32, (height * len(outs), hidden_ref.shape[0]), 0)
    place = (spot == target_ref[...]).astype(jnp.float32).astype(jnp.bfloat16)
    for part in chunks(hidden_ref.shape[1]):
        packed = jnp.dot(place, hidden_ref[:, part], preferred_element_type=jnp.float32)
        packed = packed.astype(jnp.bfloat16)
        for i, out in enumerate(outs):
            out[:, part] = packed[i * height : (i + 1) * height]


def pack_first(target, hidden, height, count):
    rows, width = hidden.shape
    return pl.pallas_call(
        pack_first_kernel,
        in_specs=[VMEM] * 2,
        out_specs=[VMEM] * count,
        out_shape=[jax.ShapeDtypeStruct((height, width), jnp.bfloat16)] * count,
        **options("first"),
    )(target.reshape(1, rows), hidden)


def expand(total, up):
    shrunk = total.astype(jnp.bfloat16)
    wide = jnp.dot(shrunk, up, preferred_element_type=jnp.float32)
    return (adapter_scale * wide).astype(jnp.bfloat16)


def shrink(row_parts, downs):
    total = None
    for part in chunks(row_parts[0].shape[1]):
        rows = jnp.concatenate([ref[:, part] for ref in row_parts], axis=0)
        down = jnp.concatenate([ref[:, part] for ref in downs], axis=0)
        product = lax.dot_general(rows, down, NT, preferred_element_type=jnp.float32)
        total = product if total is None else total + product
    return total


def put(out, dest, slots, slot, rows):
    height = rows.shape[0]
    start = pl.multiple_of((dest * slots + slot) * height, height)
    out[pl.ds(start, height), :] = rows


def join_kernel(down_hbm, up_hbm, out_ref, sems):
    width = down_hbm.shape[1]
    down = pltpu.make_async_copy(down_hbm, out_ref.at[:, :width], sems.at[0])
    up = pltpu.make_async_copy(up_hbm, out_ref.at[:, width:], sems.at[1])
    down.start()
    up.start()
    down.wait()
    up.wait()


def join(down, up):
    return pl.pallas_call(
        join_kernel,
        in_specs=[HBM] * 2,
        out_specs=VMEM,
        out_shape=jax.ShapeDtypeStruct((down.shape[0], down.shape[1] + up.shape[1]), down.dtype),
        scratch_shapes=[pltpu.SemaphoreType.DMA((2,))],
        **options("join", 1000, 60),
    )(down, up)


def early_kernel(capacity, where_ref, *refs):
    rows, (outward, middle, own, *outs) = refs[: 3 * PLANE], refs[3 * PLANE :]
    width, rank = rows[0].shape[1], own.shape[0]

    def run(weights):
        total = shrink(rows, weights)
        for slot, weight in enumerate(weights):
            start = slot * PLANE * capacity
            sums = total[start : start + PLANE * capacity, slot * rank : (slot + 1) * rank]
            wide = expand(sums, weight[:, width:])
            for k, out in enumerate(outs):
                out[slot * capacity : (slot + 1) * capacity] = wide[
                    k * capacity : (k + 1) * capacity
                ]

    pl.when(where_ref[0] == 1)(lambda: run([outward, own, middle]))
    pl.when(where_ref[0] == 0)(lambda: run([outward, own, outward]))


def early(where, rows, outward, middle, own, capacity):
    out_width = own.shape[1] - rows[0].shape[1]
    return pl.pallas_call(
        functools.partial(early_kernel, capacity),
        in_specs=[SMEM] + [VMEM] * (3 * PLANE + 3),
        out_specs=[VMEM] * PLANE,
        out_shape=[jax.ShapeDtypeStruct((3 * capacity, out_width), jnp.bfloat16)] * PLANE,
        **options("early", 1000),
    )(where, *rows, outward, middle, own)


def late_kernel(capacity, where_ref, *refs):
    rows, (middle2, swapped, out) = refs[:PLANE], refs[PLANE:]
    width = rows[0].shape[1]
    place, here, there = where_ref[1], where_ref[2], where_ref[3]

    def spread(first, wide):
        for k in range(PLANE):
            put(out, first + (place ^ k), 1, 0, wide[k * capacity : (k + 1) * capacity])

    @pl.when(where_ref[0] == 1)
    def _():
        total = shrink([*rows, swapped], [middle2])
        wide = expand(total, middle2[:, width:])
        spread(here, wide)
        spread(there, wide[PLANE * capacity :])

    @pl.when(where_ref[0] == 0)
    def _():
        wide = expand(shrink(rows, [swapped]), swapped[:, width:])
        spread(here, wide)
        spread(there, jnp.zeros(wide.shape, wide.dtype))


def late(where, rows, middle2, swapped, capacity):
    out_width = swapped.shape[1] - rows[0].shape[1]
    return pl.pallas_call(
        functools.partial(late_kernel, capacity),
        in_specs=[SMEM] + [VMEM] * (PLANE + 2),
        out_specs=VMEM,
        out_shape=jax.ShapeDtypeStruct((2 * PLANE * capacity, out_width), jnp.bfloat16),
        **options("late"),
    )(where, *rows, middle2, swapped)


def choose_kernel(where_ref, weights_hbm, *refs):
    rows, (out_hbm, stack_ref, sems) = refs[:PLANE], refs[PLANE:]
    capacity, width = stack_ref.shape[0] // PLANE, stack_ref.shape[1]

    @pl.when(where_ref[0] == 0)
    def _():
        copies = []
        for k, ref in enumerate(rows):
            for i, part in enumerate(chunks(width)):
                here = stack_ref.at[k * capacity : (k + 1) * capacity, part]
                there = out_hbm.at[k * capacity : (k + 1) * capacity, part]
                fetch = pltpu.make_async_copy(ref.at[:, part], here, sems.at[0, k, i])
                copies.append((fetch, pltpu.make_async_copy(here, there, sems.at[1, k, i])))
                fetch.start()
        for fetch, store in copies:
            fetch.wait()
            store.start()
        for _, store in copies:
            store.wait()


def choose(where, weights, rows):
    height, width = rows[0].shape
    return pl.pallas_call(
        choose_kernel,
        in_specs=[SMEM] + [HBM] * (1 + PLANE),
        out_specs=HBM,
        out_shape=jax.ShapeDtypeStruct(weights.shape, weights.dtype),
        scratch_shapes=[
            pltpu.VMEM((height * PLANE, width), weights.dtype),
            pltpu.SemaphoreType.DMA((2, PLANE, len(chunks(width)))),
        ],
        input_output_aliases={1: 0},
        **options("choose", 1000, 60),
    )(where, weights, *rows)


def by_planes(hidden, slot, down, up, capacity, meanwhile):
    devices = lax.axis_size("adapter")
    me = lax.axis_index("adapter")
    plane, place = me // PLANE, me % PLANE
    inner = (plane == 1) | (plane == 2)
    here = plane % 2 * PLANE
    where = jnp.stack([inner.astype(jnp.int32), place, here, PLANE - here]).astype(jnp.int32)
    all_devices = range(devices)
    middles = [i for i in all_devices if i // PLANE in (1, 2)]
    across = [
        [(i, (i // PLANE) * PLANE + ((i % PLANE) ^ k)) for i in all_devices] for k in range(PLANE)
    ]
    to_outward = [(i, i ^ PLANE) for i in all_devices]
    to_middle = [(i, i ^ (3 * PLANE)) for i in middles]
    send = lambda a, pairs: lax.ppermute(a, "adapter", pairs)

    def gather(rows, size):
        parts = rows.reshape(size, -1, rows.shape[1])
        groups = [list(range(i, i + size)) for i in range(0, devices, size)]
        parts = lax.all_to_all(parts, "adapter", 0, 0, axis_index_groups=groups, tiled=True)
        return parts.reshape(rows.shape)

    exchange = lambda parts: [parts[0]] + [send(parts[k], across[k]) for k in range(1, PLANE)]

    plane_of, place_of = slot // PLANE, slot % PLANE
    distance = jnp.abs(plane_of - plane)
    at_end = (plane_of == 0) | (plane_of == 3)
    kind = jnp.where(
        distance == 0,
        1,
        jnp.where(distance == 2, 3, jnp.where((distance == 3) | at_end, 0, 2)),
    )
    rank = rank_in_slot(slot)
    k = place_of ^ place
    back = jnp.where(
        kind < 3,
        (k * 3 + kind) * capacity + rank,
        (3 * PLANE + here + place_of) * capacity + rank,
    )
    passed = (3 * PLANE + PLANE - here + place_of) * capacity + rank
    back = jnp.where((kind == 0) & ~inner, passed, back)

    weights = join(down, up)
    outward, middle = send(weights, to_outward), send(weights, to_middle)
    first = pack_first(
        jnp.where(kind == 0, (k - 1) * capacity + rank, -1), hidden, capacity, PLANE - 1
    )
    to_rest = jnp.where(kind == 0, jnp.where(k == 0, 0, -1), 1 + (kind - 1) * PLANE + k)
    to_rest = jnp.where(to_rest < 0, -1, to_rest * capacity + rank)
    kept, *rest = pack(to_rest, hidden, [capacity] * (1 + 3 * PLANE), LONG)
    own, near, far = (rest[i * PLANE : (i + 1) * PLANE] for i in range(3))
    first, own = lax.optimization_barrier((exchange([kept, *first]), own))
    own = exchange(own)
    done = meanwhile()
    middle = choose(where, middle, first)
    own, near, middle = lax.optimization_barrier((own, near, middle))
    middle2, swapped = send(outward, to_middle), send(middle, to_outward)
    near, far, done = lax.optimization_barrier((exchange(near), far, done))
    far = exchange(far)
    rows = [*first, *own, *near]
    soon = early(where, rows, outward, middle, weights, capacity)
    soon, where = lax.optimization_barrier((soon, where))
    soon = exchange(soon)
    last = late(where, far, middle2, swapped, capacity)
    soon[1], soon[2], last = lax.optimization_barrier((soon[1], soon[2], last))
    last = gather(last, 2 * PLANE)
    return back, [*soon, last], done


def by_rows(hidden, slot, down, up, capacity, meanwhile):
    devices = lax.axis_size("adapter")
    target = slot * capacity + rank_in_slot(slot)
    spots = jnp.arange(devices * capacity, dtype=jnp.int32)
    placing = (target[None, :] == spots[:, None]).astype(jnp.bfloat16)
    outgoing = jnp.dot(placing, hidden, preferred_element_type=jnp.float32).astype(jnp.bfloat16)
    outgoing = outgoing.reshape(devices, capacity, hidden.shape[1])
    incoming = lax.all_to_all(outgoing, "adapter", split_axis=0, concat_axis=0, tiled=True)
    rows = incoming.reshape(-1, hidden.shape[1])
    shrunk = lax.dot_general(rows, down, NT, preferred_element_type=jnp.float32)
    wide = expand(shrunk, up)
    returned = lax.all_to_all(
        wide.reshape(devices, capacity, -1), "adapter", split_axis=0, concat_axis=0, tiled=True
    )
    return target, [returned.reshape(devices * capacity, -1)], meanwhile()


def on_device(
    hidden,
    queries,
    base_key_value,
    key_value_cache,
    lengths,
    request_adapter_index,
    adapter_position_map,
    adapter_down_weight,
    adapter_up_weight,
):
    devices = lax.axis_size("adapter")
    capacity = max(2, 2 * hidden.shape[0] // devices)
    slot = slot_lookup(request_adapter_index[:, 0], adapter_position_map)
    deliver = by_planes if devices == 4 * PLANE else by_rows
    meanwhile = lambda: cached_attention(queries, key_value_cache, lengths)
    target, pieces, (mixed, logs) = deliver(
        hidden, slot, adapter_down_weight[0], adapter_up_weight[0], capacity, meanwhile
    )
    return finish(target, base_key_value, queries, mixed, logs, pieces)


def solution(mesh):
    rows = P(("groups", "adapter"), None)
    deep = P(("groups", "adapter"), None, None)
    placed = (
        rows,
        rows,
        rows,
        deep,
        P(("groups", "adapter")),
        rows,
        P("groups"),
        deep,
        deep,
    )
    return jax.shard_map(
        on_device, mesh=mesh, in_specs=placed, out_specs=(rows, rows), check_vma=False
    )
```
